128 devices in a mesh: row: 64 (over z, y, x_hi, core), blk: 2 (over x_lo).
Axes of the slice: x: 4 (x_hi: 2, x_lo: 2; x = x_hi * 2 + x_lo), y: 4, z: 4, core: 2. Of those that a mesh axis runs over, the one named last changes fastest.
Arguments:
- field: bfloat16 [2, 256, 1024, 1024], P(None, 'blk', 'row'), may hold values from -400 to 400
- gain: float32 [256], P('blk'), may hold values from 0.1 to 1.9
- w_first: bfloat16 [2, 8, 32, 32], replicated, may hold values from -1 to 1
- b_first: float32 [2, 256], replicated, may hold values from -4 to 4
- w_second: bfloat16 [2, 8, 32, 32], replicated, may hold values from -1 to 1
- b_second: float32 [2, 256], replicated, may hold values from -4 to 4
Outputs:
- mixed: bfloat16 [2, 256, 1024, 1024], P(None, 'blk', 'row')
The draws below stay inside these ranges and needn't reach their ends.
All inputs are finite; a program needn't handle non-finite values.
Results may differ from the reference program's by a relative error of at most 0.02.
Values may be sent and summed in bfloat16 or wider, within the bound.
No kernel may reach another device: no remote copies, remote signals or barrier semaphores. Data moves between devices by JAX's collectives and lax.ppermute only.
A program may use at most 128 MiB of HBM per device.

```python
import math
import jax
import jax.numpy as jnp
from jax import lax

SLICES = 2
CHANNELS = 256
BLOCKS = 8
BLOCK_CH = 32
HEIGHT = 1024
COLUMNS = 1024
MODES_Y = 512
MODES_X = 128


def draw_field(key, part):
    key = jax.random.fold_in(key, 7)
    key_noise, key_chan, key_pixel = jax.random.split(key, 3)
    shape_all = (SLICES, CHANNELS, HEIGHT, COLUMNS)
    chan_pos = jnp.arange(CHANNELS, dtype=jnp.float32) / CHANNELS
    noise = jnp.clip(jax.random.normal(key_noise, shape_all, jnp.float32), -6.0, 6.0)
    chan_scale = jnp.power(10.0, 0.6 * chan_pos + 0.4 * jax.random.uniform(key_chan, (CHANNELS,), jnp.float32))
    pixel_scale = jnp.power(10.0, 0.5 * jax.random.uniform(key_pixel, (SLICES, 1, HEIGHT, COLUMNS), jnp.float32))
    result = noise * chan_scale[:, None, None] * pixel_scale
    return result.astype(jnp.bfloat16)


def scatter_about(stream_key, shape, spread, limit, held_as=jnp.bfloat16):
    values = spread * jax.random.normal(stream_key, shape, jnp.float32)
    return jnp.clip(values, min=-limit, max=limit).astype(held_as)


def setup_inputs(seed: int = 0) -> dict:
    streams_of = jax.random.split(jax.random.key(seed), 7)
    field = draw_field(jax.random.fold_in(streams_of[6], 71), 0)
    gain = jnp.clip(1.0 + 0.18 * jax.random.normal(streams_of[1], (CHANNELS,), jnp.float32), 0.1, 1.9)
    w_first = scatter_about(streams_of[2], (2, BLOCKS, BLOCK_CH, BLOCK_CH), BLOCK_CH ** -0.5, 1.0)
    b_first = scatter_about(streams_of[3], (2, CHANNELS), 0.3, 4.0, jnp.float32)
    w_second = scatter_about(streams_of[4], (2, BLOCKS, BLOCK_CH, BLOCK_CH), BLOCK_CH ** -0.5, 1.0)
    b_second = scatter_about(streams_of[5], (2, CHANNELS), 0.3, 4.0, jnp.float32)
    return {"field": field, "gain": gain, "w_first": w_first, "b_first": b_first, "w_second": w_second, "b_second": b_second}


EPS = 1e-05
SHRINK = 0.01

def forward_table(count):
    positions = jnp.arange(count, dtype=jnp.int32)[:, None]
    freqs = jnp.arange(MODES_X, dtype=jnp.int32)[None, :]
    radians = (positions * freqs % count).astype(jnp.float32) * (2.0 * math.pi / count)
    norm_scale = 1.0 / math.sqrt(count)
    return jnp.stack([jnp.cos(radians) * norm_scale, -jnp.sin(radians) * norm_scale], axis=1).astype(jnp.bfloat16)

def inverse_table(count):
    freqs = jnp.arange(MODES_X, dtype=jnp.int32)[:, None]
    positions = jnp.arange(count, dtype=jnp.int32)[None, :]
    radians = (positions * freqs % count).astype(jnp.float32) * (2.0 * math.pi / count)
    weight_k = jnp.where(freqs == 0, 1.0, 2.0).astype(jnp.float32) / math.sqrt(count)
    return jnp.stack([jnp.cos(radians) * weight_k, -jnp.sin(radians) * weight_k], axis=0).astype(jnp.bfloat16)

def height_matrix(positions):
    mode_index = jnp.arange(MODES_Y, dtype=jnp.int32) - MODES_Y // 2
    phase_int = mode_index[:, None] * positions[None, :] % HEIGHT
    radians = phase_int.astype(jnp.float32) * (2.0 * math.pi / HEIGHT)
    norm_scale = 1.0 / math.sqrt(HEIGHT)
    cosine = (jnp.cos(radians) * norm_scale).astype(jnp.bfloat16)
    sine_part = (jnp.sin(radians) * norm_scale).astype(jnp.bfloat16)
    upper_rows = jnp.concatenate([cosine, sine_part], axis=1)
    lower_rows = jnp.concatenate([-sine_part, cosine], axis=1)
    return jnp.concatenate([upper_rows, lower_rows], axis=0)

def block_filter(real_spec, imag_spec, first_w, first_b, second_w, second_b):

    def mix_channels(values_in, weights):
        return jnp.einsum('mbjik,jio->mbjok', values_in, weights, precision=lax.Precision.HIGHEST)

    def widen_bias(vector):
        return vector[None, None, :, :, None]
    real_hidden = jax.nn.relu(mix_channels(real_spec, first_w[0]) - mix_channels(imag_spec, first_w[1]) + widen_bias(first_b[0]))
    imag_hidden = jax.nn.relu(mix_channels(imag_spec, first_w[0]) + mix_channels(real_spec, first_w[1]) + widen_bias(first_b[1]))
    real_out = mix_channels(real_hidden, second_w[0]) - mix_channels(imag_hidden, second_w[1]) + widen_bias(second_b[0])
    imag_out = mix_channels(imag_hidden, second_w[0]) + mix_channels(real_hidden, second_w[1]) + widen_bias(second_b[1])
    stacked = jnp.stack([real_out, imag_out])
    return (stacked - jnp.clip(stacked, -SHRINK, SHRINK)).astype(jnp.bfloat16)

def reference(field, gain, w_first, b_first, w_second, b_second):
    widened = field.astype(jnp.float32)
    average = lax.optimization_barrier(jnp.mean(widened, axis=1, keepdims=True))
    centered = widened - average
    variance = lax.optimization_barrier(jnp.mean(centered * centered, axis=1, keepdims=True))
    normed = (centered * lax.rsqrt(variance + EPS) * gain[None, :, None, None]).astype(jnp.bfloat16)
    forward = forward_table(COLUMNS).astype(jnp.float32)
    inverse = inverse_table(COLUMNS).astype(jnp.float32)
    matrix = height_matrix(jnp.arange(HEIGHT, dtype=jnp.int32))
    mat_fwd = matrix.astype(jnp.float32).reshape(2, MODES_Y, 2, HEIGHT)
    mat_inv = matrix.T.astype(jnp.float32).reshape(2, HEIGHT, 2, MODES_Y)
    grouped = jnp.moveaxis(normed.reshape(SLICES, BLOCKS, BLOCK_CH, HEIGHT, COLUMNS), 1, 0)
    first_w = jnp.moveaxis(w_first, 1, 0).astype(jnp.float32)
    second_w = jnp.moveaxis(w_second, 1, 0).astype(jnp.float32)
    first_b = jnp.moveaxis(b_first.reshape(2, BLOCKS, BLOCK_CH), 1, 0)
    second_b = jnp.moveaxis(b_second.reshape(2, BLOCKS, BLOCK_CH), 1, 0)
    highest = lax.Precision.HIGHEST

    def one_block(inputs):
        block_field, weight_one, bias_one, weight_two, bias_two = inputs
        rowspec = jnp.einsum('bchw,wrk->rbchk', block_field.astype(jnp.float32), forward, precision=highest).astype(jnp.bfloat16)
        spectrum = jnp.einsum('smrh,rbchk->smbck', mat_fwd, rowspec.astype(jnp.float32), precision=highest)
        shaped = spectrum.reshape(2, MODES_Y, SLICES, 1, BLOCK_CH, MODES_X)
        filtered = block_filter(shaped[0], shaped[1], weight_one[:, None], bias_one[:, None], weight_two[:, None], bias_two[:, None])
        filtered = filtered.reshape(2, MODES_Y, SLICES, BLOCK_CH, MODES_X)
        colfield = jnp.einsum('rhsm,smbck->rbchk', mat_inv, filtered.astype(jnp.float32), precision=highest).astype(jnp.bfloat16)
        return jnp.einsum('rbchk,rkw->bchw', colfield.astype(jnp.float32), inverse, precision=highest).astype(jnp.bfloat16)
    outputs = lax.map(one_block, (grouped, first_w, first_b, second_w, second_b))
    return jnp.moveaxis(outputs, 0, 1).reshape(SLICES, CHANNELS, HEIGHT, COLUMNS)
```

```python
import functools
import math

import jax
import jax.numpy as jnp
import ml_dtypes
import numpy as np
from jax import lax
from jax.experimental import pallas as pl
from jax.experimental.pallas import tpu as pltpu
from jax.sharding import PartitionSpec as P

BLOCK_CH = 32
EPS = 1e-05
SHRINK = 0.01
LANES = 128
BF16 = jnp.bfloat16
F32 = jnp.float32
MIB = 1 << 20


def _angles(first, second, count):
    phase = np.mod(np.outer(first, second), count)
    return phase.astype(np.float32) * np.float32(2.0 * math.pi / count)


def _bf16(values):
    return np.asarray(values, np.float32).astype(ml_dtypes.bfloat16)


def forward_table(count, modes):
    t = _angles(np.arange(count), np.arange(modes), count)
    scale = np.float32(1.0 / math.sqrt(count))
    return _bf16(np.concatenate([np.cos(t) * scale, -np.sin(t) * scale], axis=1))


def inverse_table(count, modes):
    t = _angles(np.arange(modes), np.arange(count), count)
    weight = np.where(np.arange(modes) == 0, 1.0, 2.0)[:, None].astype(np.float32)
    weight = weight * np.float32(1.0 / math.sqrt(count))
    return _bf16(np.concatenate([np.cos(t) * weight, -np.sin(t) * weight], axis=0))


def height_tables(height):
    modes = height // 2
    s = _angles(np.arange(modes) - modes // 2, np.arange(height), height)
    scale = np.float32(1.0 / math.sqrt(height))
    cosine, sine = np.cos(s) * scale, np.sin(s) * scale
    return _bf16(np.concatenate([cosine, sine], axis=0)), _bf16(
        np.concatenate([cosine.T, sine.T], axis=1)
    )


def stats_kernel(x_ref, out_ref):
    channels = x_ref.shape[1]
    zero = jnp.zeros(x_ref.shape[2:], F32)

    def add(c, total):
        return total + x_ref[0, c].astype(F32)

    mean = lax.fori_loop(0, channels, add, zero, unroll=16) * (1.0 / channels)

    def add_square(c, total):
        centered = x_ref[0, c].astype(F32) - mean
        return total + centered * centered

    moment = lax.fori_loop(0, channels, add_square, zero, unroll=16)
    high = mean.astype(BF16)
    out_ref[0] = high
    out_ref[1] = (mean - high.astype(F32)).astype(BF16)
    out_ref[2] = moment.astype(BF16)


def channel_stats(field, which):
    _, channels, rows, width = field.shape
    wide = min(256, width)
    return pl.pallas_call(
        stats_kernel,
        grid=(width // wide,),
        in_specs=[pl.BlockSpec((1, channels, rows, wide), lambda j: (which, 0, 0, j))],
        out_specs=pl.BlockSpec((3, rows, wide), lambda j: (0, 0, j)),
        out_shape=jax.ShapeDtypeStruct((3, rows, width), BF16),
        compiler_params=pltpu.CompilerParams(vmem_limit_bytes=16 * MIB),
        cost_estimate=pl.CostEstimate(
            flops=5 * channels * rows * width, bytes_accessed=2 * channels * rows * width, transcendentals=0
        ),
        name="channel_stats",
    )(field)


def forward_kernel(chan_block, gain_ref, x_ref, own_ref, other_ref, table_ref, eye_ref, *rest):
    send_ref, mean_s, scale_s, spec_s, turn_s = rest[-5:]
    step = pl.program_id(0)
    rows = x_ref.shape[2]
    channels = spec_s.shape[1] // rows
    two_k = table_ref.shape[1]
    half = spec_s.shape[2]
    parts = spec_s.shape[0]

    @pl.when(step == 0)
    def _():
        own_mean = own_ref[0].astype(F32) + own_ref[1].astype(F32)
        other_mean = other_ref[0].astype(F32) + other_ref[1].astype(F32)
        delta = own_mean - other_mean
        total = 2.0 * channels
        moment = own_ref[2].astype(F32) + other_ref[2].astype(F32) + delta * delta * (channels * 0.5)
        mean_s[...] = (own_mean + other_mean) * 0.5
        scale_s[...] = lax.rsqrt(moment * (1.0 / total) + EPS)

    mean = mean_s[...][None]
    scale = scale_s[...][None]
    normed = ((x_ref[0].astype(F32) - mean) * scale).astype(BF16)
    spec = jnp.dot(normed.reshape(chan_block * rows, -1), table_ref[...], preferred_element_type=F32)
    for c in range(chan_block):
        scaled = spec[c * rows : (c + 1) * rows] * gain_ref[step * chan_block + c]
        start = pl.multiple_of(step * (chan_block * rows), chan_block * rows) + c * rows
        for p in range(parts):
            spec_s[p, pl.ds(start, rows), :] = scaled[:, p * half : (p + 1) * half]

    @pl.when(step == pl.num_programs(0) - 1)
    def _():
        per_part = half
        for h in range(rows):
            for p in range(parts):
                picked = spec_s[p, pl.ds(h, channels, stride=rows), :].astype(BF16)
                turned = lax.dot_general(
                    eye_ref[...], picked, (((1,), (1,)), ((), ())), preferred_element_type=F32
                )
                turn_s[pl.ds(p * per_part * rows + h, per_part, stride=rows), :] = turned
        owners = send_ref.shape[1]
        lanes = turn_s.shape[1]
        for r in range(2):
            chunk = turn_s[r * (two_k // 2) * rows : (r + 1) * (two_k // 2) * rows, :]
            chunk = chunk.astype(BF16).reshape(owners, 2, rows, lanes)
            for kk in range(2):
                send_ref[0, :, r * rows : (r + 1) * rows, kk * lanes : (kk + 1) * lanes] = chunk[:, kk]


def forward_slice(field, which, gain, own, other, table, eye, owners, send):
    slices, channels, rows, width = field.shape
    two_k = table.shape[1]
    half = eye.shape[0]
    chan_block = min(32, channels)
    aliased = [] if send is None else [send]
    return pl.pallas_call(
        functools.partial(forward_kernel, chan_block),
        grid=(channels // chan_block,),
        in_specs=[
            pl.BlockSpec(memory_space=pltpu.SMEM),
            pl.BlockSpec((1, chan_block, rows, width), lambda i: (which, i, 0, 0)),
            pl.BlockSpec((3, rows, width), lambda i: (0, 0, 0)),
            pl.BlockSpec((3, rows, width), lambda i: (0, 0, 0)),
            pl.BlockSpec((width, two_k), lambda i: (0, 0)),
            pl.BlockSpec((half, half), lambda i: (0, 0)),
        ]
        + [pl.BlockSpec(memory_space=pl.ANY) for _ in aliased],
        out_specs=pl.BlockSpec((1, owners, 2 * rows, 2 * channels), lambda i: (which, 0, 0, 0)),
        out_shape=jax.ShapeDtypeStruct((slices, owners, 2 * rows, 2 * channels), BF16),
        scratch_shapes=[
            pltpu.VMEM((rows, width), F32),
            pltpu.VMEM((rows, width), F32),
            pltpu.VMEM((two_k // half, channels * rows, half), F32),
            pltpu.VMEM((two_k * rows, channels), F32),
        ],
        input_output_aliases={6: 0} if aliased else {},
        compiler_params=pltpu.CompilerParams(vmem_limit_bytes=24 * MIB),
        cost_estimate=pl.CostEstimate(
            flops=2 * channels * rows * width * two_k,
            bytes_accessed=2 * channels * rows * width,
            transcendentals=0,
        ),
        name="norm_and_row_dft",
    )(gain, field, own, other, table, eye, *aliased)


def block_diagonal(weights, spread, lanes):
    tiled = jnp.dot(weights, spread, preferred_element_type=F32)
    row = lax.broadcasted_iota(jnp.int32, (lanes, lanes), 0) // BLOCK_CH
    col = lax.broadcasted_iota(jnp.int32, (lanes, lanes), 1) // BLOCK_CH
    return jnp.where(row == col, tiled, 0.0)


def fill_weights(w_ref, spread, big, lanes):
    big[...] = jnp.zeros(big.shape, big.dtype)
    real = block_diagonal(w_ref[0], spread, lanes)
    imag = block_diagonal(w_ref[1], spread, lanes)
    for kk in range(2):
        for part_in in range(2):
            for part_out in range(2):
                if part_in == part_out:
                    block = real
                else:
                    block = imag if part_in == 0 else -imag
                row = (part_in * 2 + kk) * lanes
                col = (part_out * 2 + kk) * lanes
                big[row : row + lanes, col : col + lanes] = block.astype(big.dtype)


def bias_row(b_ref):
    parts = [b_ref[0, 0:1], b_ref[0, 0:1], b_ref[0, 1:2], b_ref[0, 1:2]]
    return jnp.concatenate(parts, axis=1)


def filter_kernel(x_ref, fwd_ref, inv_ref, spread_ref, w1_ref, b1_ref, w2_ref, b2_ref, out_ref, big1, big2, turned):
    owners, two_rows, wide = x_ref.shape[1:]
    rows = two_rows // 2
    lanes = wide // 2
    height = owners * rows
    modes = height // 2
    fill_weights(w1_ref, spread_ref[...], big1, lanes)
    fill_weights(w2_ref, spread_ref[...], big2, lanes)

    real_in = x_ref[0, :, :rows, :].reshape(height, wide)
    imag_in = x_ref[0, :, rows:, :].reshape(height, wide)
    from_real = jnp.dot(fwd_ref[...], real_in, preferred_element_type=F32)
    from_imag = jnp.dot(fwd_ref[...], imag_in, preferred_element_type=F32)
    real = (from_real[:modes] + from_imag[modes:]).astype(BF16)
    imag = (from_imag[:modes] - from_real[modes:]).astype(BF16)
    spectrum = jnp.concatenate([real, imag], axis=1)
    hidden = jnp.dot(spectrum, big1[...], preferred_element_type=F32) + bias_row(b1_ref)
    hidden = jnp.maximum(hidden, 0.0).astype(BF16)
    mixed = jnp.dot(hidden, big2[...], preferred_element_type=F32) + bias_row(b2_ref)
    kept = (mixed - jnp.clip(mixed, -SHRINK, SHRINK)).astype(BF16)
    turned[:modes, :] = kept
    turned[modes:, :wide] = -kept[:, wide:]
    turned[modes:, wide:] = kept[:, :wide]
    column = jnp.dot(inv_ref[...], turned[...], preferred_element_type=F32).astype(BF16)
    out_ref[0, :, :rows, :] = column[:, :wide].reshape(owners, rows, wide)
    out_ref[0, :, rows:, :] = column[:, wide:].reshape(owners, rows, wide)


def filter_columns(received, fwd, inv, spread, w_first, b_first, w_second, b_second):
    groups, owners, two_rows, wide = received.shape
    lanes = wide // 2
    height = owners * two_rows // 2
    whole = lambda a: (0, 0)
    weights = pl.BlockSpec((2, lanes, BLOCK_CH), lambda a: (0, a, 0))
    bias = pl.BlockSpec((1, 2, lanes), lambda a: (a, 0, 0))
    block = pl.BlockSpec((1, owners, two_rows, wide), lambda a: (a, 0, 0, 0))

    def flat(w):
        return w.reshape(2, -1, BLOCK_CH)

    def grouped(b):
        return jnp.swapaxes(b.reshape(2, groups, lanes), 0, 1)

    return pl.pallas_call(
        filter_kernel,
        grid=(groups,),
        in_specs=[
            block,
            pl.BlockSpec(fwd.shape, whole),
            pl.BlockSpec(inv.shape, whole),
            pl.BlockSpec(spread.shape, whole),
            weights,
            bias,
            weights,
            bias,
        ],
        out_specs=block,
        out_shape=jax.ShapeDtypeStruct(received.shape, BF16),
        scratch_shapes=[
            pltpu.VMEM((2 * wide, 2 * wide), BF16),
            pltpu.VMEM((2 * wide, 2 * wide), BF16),
            pltpu.VMEM((height, 2 * wide), BF16),
        ],
        compiler_params=pltpu.CompilerParams(vmem_limit_bytes=40 * MIB),
        cost_estimate=pl.CostEstimate(
            flops=2 * groups * height * wide * 5 * height, bytes_accessed=8 * MIB, transcendentals=0
        ),
        name="column_filter",
    )(received, fwd, inv, spread, flat(w_first), grouped(b_first), flat(w_second), grouped(b_second))


def inverse_kernel(chan_block, x_ref, table_ref, eye_ref, out_ref, turn_s, spec_s):
    owners, two_rows, wide = x_ref.shape[1:]
    rows = two_rows // 2
    lanes = wide // 2
    channels = spec_s.shape[1] // rows
    parts, _, half = spec_s.shape
    step = pl.program_id(1)

    @pl.when(step == 0)
    def _():
        for r in range(2):
            pair = [
                x_ref[0, :, r * rows : (r + 1) * rows, kk * lanes : (kk + 1) * lanes][:, None]
                for kk in range(2)
            ]
            block = jnp.concatenate(pair, axis=1).astype(F32)
            size = owners * 2 * rows
            turn_s[r * size : (r + 1) * size, :] = block.reshape(size, lanes)
        for h in range(rows):
            for p in range(parts):
                picked = turn_s[pl.ds(p * half * rows + h, half, stride=rows), :].astype(BF16)
                turned = lax.dot_general(
                    eye_ref[...], picked, (((1,), (1,)), ((), ())), preferred_element_type=F32
                )
                spec_s[p, pl.ds(h, channels, stride=rows), :] = turned

    size = chan_block * rows
    start = pl.multiple_of(step * size, size)
    spec = jnp.concatenate([spec_s[p, pl.ds(start, size), :].astype(BF16) for p in range(parts)], axis=1)
    mixed = jnp.dot(spec, table_ref[...], preferred_element_type=F32)
    out_ref[0] = mixed.astype(BF16).reshape(chan_block, rows, -1)


def inverse_rows(received, table, eye):
    slices, owners, two_rows, wide = received.shape
    rows = two_rows // 2
    channels = wide // 2
    two_k, width = table.shape
    half = two_k // 2
    chan_block = min(32, channels)
    return pl.pallas_call(
        functools.partial(inverse_kernel, chan_block),
        grid=(slices, channels // chan_block),
        in_specs=[
            pl.BlockSpec((1, owners, two_rows, wide), lambda b, i: (b, 0, 0, 0)),
            pl.BlockSpec(table.shape, lambda b, i: (0, 0)),
            pl.BlockSpec(eye.shape, lambda b, i: (0, 0)),
        ],
        out_specs=pl.BlockSpec((1, chan_block, rows, width), lambda b, i: (b, i, 0, 0)),
        out_shape=jax.ShapeDtypeStruct((slices, channels, rows, width), BF16),
        scratch_shapes=[
            pltpu.VMEM((two_k * rows, channels), F32),
            pltpu.VMEM((2, channels * rows, half), F32),
        ],
        compiler_params=pltpu.CompilerParams(vmem_limit_bytes=24 * MIB),
        cost_estimate=pl.CostEstimate(
            flops=2 * slices * channels * rows * width * two_k,
            bytes_accessed=2 * slices * channels * rows * width,
            transcendentals=0,
        ),
        name="inverse_row_dft",
    )(received, table, eye)


def exchange(blocks):
    shape = blocks.shape
    flat = blocks.reshape((shape[0] * shape[1],) + shape[2:])
    flat = lax.all_to_all(flat, ("blk", "row"), split_axis=0, concat_axis=0, tiled=True)
    return flat.reshape(shape)


def local(field, gain, w_first, b_first, w_second, b_second):
    slices, channels, rows, width = field.shape
    owners = lax.axis_size("row")
    modes_x = 2 * owners
    height = owners * rows
    fwd, inv = height_tables(height)
    eye_k = jnp.asarray(np.eye(modes_x), BF16)
    eye_c = jnp.asarray(np.eye(channels), BF16)
    spread = jnp.asarray(np.tile(np.eye(BLOCK_CH), (1, channels // BLOCK_CH)), BF16)
    table = jnp.asarray(forward_table(width, modes_x))

    swap = [(0, 1), (1, 0)]
    own = [channel_stats(field, b) for b in range(slices)]
    other = [lax.ppermute(s, "blk", swap) for s in own]
    send = None
    for b in range(slices):
        send = forward_slice(field, b, gain, own[b], other[b], table, eye_k, owners, send)
    columns = exchange(send)
    filtered = filter_columns(
        columns, jnp.asarray(fwd), jnp.asarray(inv), spread, w_first, b_first, w_second, b_second
    )
    colfield = exchange(filtered)
    return inverse_rows(colfield, jnp.asarray(inverse_table(width, modes_x)), eye_c)


def solution(mesh):
    return jax.shard_map(
        local,
        mesh=mesh,
        in_specs=(P(None, "blk", "row", None), P("blk"), P(), P(), P(), P()),
        out_specs=P(None, "blk", "row", None),
        check_vma=False,
    )
```

```python
import functools
import math

import jax
import jax.numpy as jnp
import ml_dtypes
import numpy as np
from jax import lax
from jax.experimental import pallas as pl
from jax.experimental.pallas import tpu as pltpu
from jax.sharding import PartitionSpec as P

BLOCK_CH = 32
EPS = 1e-05
SHRINK = 0.01
LANES = 128
BF16 = jnp.bfloat16
F32 = jnp.float32
MIB = 1 << 20


def _angles(first, second, count):
    phase = np.mod(np.outer(first, second), count)
    return phase.astype(np.float32) * np.float32(2.0 * math.pi / count)


def _bf16(values):
    return np.asarray(values, np.float32).astype(ml_dtypes.bfloat16)


def mode_order(modes):
    return np.arange(modes).reshape(-1, 2).T.reshape(-1)


def forward_table(count, modes):
    t = _angles(np.arange(count), mode_order(modes), count)
    scale = np.float32(1.0 / math.sqrt(count))
    return _bf16(np.concatenate([np.cos(t) * scale, -np.sin(t) * scale], axis=1))


def inverse_table(count, modes):
    order = mode_order(modes)
    t = _angles(order, np.arange(count), count)
    weight = np.where(order == 0, 1.0, 2.0)[:, None].astype(np.float32)
    weight = weight * np.float32(1.0 / math.sqrt(count))
    return _bf16(np.concatenate([np.cos(t) * weight, -np.sin(t) * weight], axis=0))


def height_tables(height):
    quarter = height // 4
    s = _angles(np.arange(quarter + 1), np.arange(height), height)
    scale = np.float32(1.0 / math.sqrt(height))
    cosine, sine = np.cos(s) * scale, np.sin(s) * scale
    last = np.zeros((16, height), np.float32)
    last[0], last[1] = cosine[quarter], sine[quarter]
    forward = np.concatenate([cosine[:quarter], sine[:quarter], last], axis=0)
    inverse = np.concatenate([cosine[:quarter].T, sine[:quarter].T], axis=1)
    return _bf16(forward), _bf16(inverse)


def stats_kernel(x_ref, out_ref):
    channels = x_ref.shape[1]
    zero = jnp.zeros(x_ref.shape[2:], F32)

    def add(c, total):
        return total + x_ref[0, c].astype(F32)

    mean = lax.fori_loop(0, channels, add, zero, unroll=16) * (1.0 / channels)

    def add_square(c, total):
        centered = x_ref[0, c].astype(F32) - mean
        return total + centered * centered

    moment = lax.fori_loop(0, channels, add_square, zero, unroll=16)
    high = mean.astype(BF16)
    out_ref[0] = high
    out_ref[1] = (mean - high.astype(F32)).astype(BF16)
    out_ref[2] = moment.astype(BF16)


def channel_stats(field, which):
    _, channels, rows, width = field.shape
    wide = min(256, width)
    return pl.pallas_call(
        stats_kernel,
        grid=(width // wide,),
        in_specs=[pl.BlockSpec((1, channels, rows, wide), lambda j: (which, 0, 0, j))],
        out_specs=pl.BlockSpec((3, rows, wide), lambda j: (0, 0, j)),
        out_shape=jax.ShapeDtypeStruct((3, rows, width), BF16),
        compiler_params=pltpu.CompilerParams(vmem_limit_bytes=16 * MIB),
        cost_estimate=pl.CostEstimate(
            flops=5 * channels * rows * width, bytes_accessed=2 * channels * rows * width, transcendentals=0
        ),
        name="channel_stats",
    )(pltpu.with_memory_space_constraint(field, pltpu.HBM))


def forward_kernel(which, pitch, x_ref, gain_ref, own_ref, other_ref, table_ref, *rest):
    send_ref, mean_s, scale_s, spec_s, turn_s = rest[-5:]
    step = pl.program_id(0)
    chan_block, rows, width = x_ref.shape[1:]
    parts, _, half = spec_s.shape
    channels = turn_s.shape[-1]
    owners = send_ref.shape[1]

    @pl.when(step == 0)
    def _():
        own_mean = own_ref[0].astype(F32) + own_ref[1].astype(F32)
        other_mean = other_ref[0].astype(F32) + other_ref[1].astype(F32)
        delta = own_mean - other_mean
        total = 2.0 * channels
        moment = own_ref[2].astype(F32) + other_ref[2].astype(F32) + delta * delta * (channels * 0.5)
        mean_s[...] = (own_mean + other_mean) * 0.5
        scale_s[...] = lax.rsqrt(moment * (1.0 / total) + EPS)

    normed = ((x_ref[0].astype(F32) - mean_s[...][None]) * scale_s[...][None]).astype(BF16)
    spec = jnp.dot(normed.reshape(chan_block * rows, width), table_ref[...], preferred_element_type=F32)
    for c in range(chan_block):
        start = pl.multiple_of(step * (chan_block * pitch), chan_block * pitch) + c * pitch
        for p in range(parts):
            spec_s[p, pl.ds(start, rows), :] = spec[c * rows : (c + 1) * rows, p * half : (p + 1) * half]

    @pl.when(step == pl.num_programs(0) - 1)
    def _():
        for h in range(rows):
            for p in range(parts):
                turned = spec_s[p, pl.ds(h, channels, stride=pitch), :].T * gain_ref[...]
                turn_s[pl.ds(p * half * pitch + h, half, stride=pitch), :] = turned
        for r in range(2):
            for kk in range(2):
                for d in range(owners):
                    start = ((r * 2 + kk) * owners + d) * pitch
                    send_ref[which, d, r * rows : (r + 1) * rows, kk * channels : (kk + 1) * channels] = turn_s[
                        start : start + rows, :
                    ].astype(BF16)


def forward_slice(field, which, gain, own, other, table, owners, send):
    slices, channels, rows, width = field.shape
    two_k = table.shape[1]
    chan_block = min(32, channels)
    pitch = rows + 8
    aliased = [] if send is None else [send]
    vmem = pl.BlockSpec(memory_space=pltpu.VMEM)
    return pl.pallas_call(
        functools.partial(forward_kernel, which, pitch),
        grid=(channels // chan_block,),
        in_specs=[pl.BlockSpec((1, chan_block, rows, width), lambda i: (which, i, 0, 0))]
        + [vmem] * (4 + len(aliased)),
        out_specs=vmem,
        out_shape=jax.ShapeDtypeStruct((slices, owners, 2 * rows, 2 * channels), BF16),
        scratch_shapes=[
            pltpu.VMEM((rows, width), F32),
            pltpu.VMEM((rows, width), F32),
            pltpu.VMEM((2, channels * pitch, two_k // 2), F32),
            pltpu.VMEM((two_k * pitch, channels), F32),
        ],
        input_output_aliases={5: 0} if aliased else {},
        compiler_params=pltpu.CompilerParams(vmem_limit_bytes=24 * MIB),
        cost_estimate=pl.CostEstimate(
            flops=2 * channels * rows * width * two_k,
            bytes_accessed=2 * channels * rows * width,
            transcendentals=0,
        ),
        name="norm_and_row_dft",
    )(pltpu.with_memory_space_constraint(field, pltpu.HBM), gain.reshape(1, channels), own, other, table, *aliased)


def block_diagonal(weights, spread, lanes):
    tiled = jnp.dot(weights, spread, preferred_element_type=F32)
    row = lax.broadcasted_iota(jnp.int32, (lanes, lanes), 0) // BLOCK_CH
    col = lax.broadcasted_iota(jnp.int32, (lanes, lanes), 1) // BLOCK_CH
    return jnp.where(row == col, tiled, 0.0)


def fill_weights(w_ref, group, spread, big, lanes):
    mine = slice(group * lanes, (group + 1) * lanes)
    real = block_diagonal(w_ref[0, mine, :], spread, lanes)
    imag = block_diagonal(w_ref[1, mine, :], spread, lanes)
    big[:lanes, :lanes] = real.astype(BF16)
    big[:lanes, lanes:] = imag.astype(BF16)
    big[lanes:, :lanes] = (-imag).astype(BF16)
    big[lanes:, lanes:] = real.astype(BF16)


def bias_row(b_ref, group, lanes):
    mine = slice(group * lanes, (group + 1) * lanes)
    return jnp.concatenate([b_ref[0:1, mine], b_ref[1:2, mine]], axis=1)


def filter_kernel(x_ref, fwd_ref, inv_ref, spread_ref, w1_ref, b1_ref, w2_ref, b2_ref, out_ref, big1, big2, packed):
    groups, owners, two_rows, wide = x_ref.shape
    rows = two_rows // 2
    lanes = wide // 2
    height = owners * rows
    quarter = height // 4
    top = lax.broadcasted_iota(jnp.int32, (quarter, lanes), 0) == 0
    turn = lax.broadcasted_iota(jnp.int32, (8, 1), 0) % 4
    norm = 1.0 / math.sqrt(height)
    last_cos = jnp.where(turn == 0, norm, jnp.where(turn == 2, -norm, 0.0))
    last_sin = jnp.where(turn == 1, norm, jnp.where(turn == 3, -norm, 0.0))
    for group in range(groups):
        fill_weights(w1_ref, group, spread_ref[...], big1, lanes)
        fill_weights(w2_ref, group, spread_ref[...], big2, lanes)
        bias1 = bias_row(b1_ref, group, lanes)
        bias2 = bias_row(b2_ref, group, lanes)
        real_in = x_ref[group, :, :rows, :].reshape(height, wide)
        imag_in = x_ref[group, :, rows:, :].reshape(height, wide)
        from_real = jnp.dot(fwd_ref[...], real_in, preferred_element_type=F32)
        from_imag = jnp.dot(fwd_ref[...], imag_in, preferred_element_type=F32)
        extra = []
        for kk in range(2):
            part = slice(kk * lanes, (kk + 1) * lanes)
            cos_re, sin_re = from_real[:quarter, part], from_real[quarter : 2 * quarter, part]
            cos_im, sin_im = from_imag[:quarter, part], from_imag[quarter : 2 * quarter, part]
            last_re = from_real[2 * quarter : 2 * quarter + 1, part] - from_imag[2 * quarter + 1 : 2 * quarter + 2, part]
            last_im = from_imag[2 * quarter : 2 * quarter + 1, part] + from_real[2 * quarter + 1 : 2 * quarter + 2, part]
            plus = jnp.concatenate([cos_re + sin_im, cos_im - sin_re], axis=1)
            minus = jnp.concatenate(
                [jnp.where(top, last_re, cos_re - sin_im), jnp.where(top, last_im, cos_im + sin_re)], axis=1
            )
            spectrum = jnp.concatenate([plus, minus], axis=0).astype(BF16)
            hidden = jnp.dot(spectrum, big1[...], preferred_element_type=F32) + bias1
            hidden = jnp.maximum(hidden, 0.0).astype(BF16)
            mixed = jnp.dot(hidden, big2[...], preferred_element_type=F32) + bias2
            kept = mixed - jnp.clip(mixed, -SHRINK, SHRINK)
            plus_re, plus_im = kept[:quarter, :lanes], kept[:quarter, lanes:]
            minus_re, minus_im = kept[quarter:, :lanes], kept[quarter:, lanes:]
            last_re, last_im = minus_re[0:1], minus_im[0:1]
            minus_re = jnp.where(top, 0.0, minus_re)
            minus_im = jnp.where(top, 0.0, minus_im)
            packed[:quarter, part] = (plus_re + minus_re).astype(BF16)
            packed[:quarter, wide + kk * lanes : wide + (kk + 1) * lanes] = (plus_im + minus_im).astype(BF16)
            packed[quarter:, part] = (minus_im - plus_im).astype(BF16)
            packed[quarter:, wide + kk * lanes : wide + (kk + 1) * lanes] = (plus_re - minus_re).astype(BF16)
            extra.append((last_cos * last_re + last_sin * last_im, last_cos * last_im - last_sin * last_re))
        column = jnp.dot(inv_ref[...], packed[...], preferred_element_type=F32)
        extra = jnp.concatenate([extra[0][0], extra[1][0], extra[0][1], extra[1][1]], axis=1)
        column = (column.reshape(height // 8, 8, 2 * wide) + extra[None]).astype(BF16)
        column = column.reshape(height, 2 * wide)
        out_ref[group, :, :rows, :] = column[:, :wide].reshape(owners, rows, wide)
        out_ref[group, :, rows:, :] = column[:, wide:].reshape(owners, rows, wide)


def filter_columns(received, fwd, inv, spread, w_first, b_first, w_second, b_second):
    groups, owners, two_rows, wide = received.shape
    height = owners * two_rows // 2
    vmem = pl.BlockSpec(memory_space=pltpu.VMEM)

    def flat(w):
        return w.reshape(2, -1, BLOCK_CH)

    return pl.pallas_call(
        filter_kernel,
        in_specs=[vmem] * 8,
        out_specs=vmem,
        out_shape=jax.ShapeDtypeStruct(received.shape, BF16),
        scratch_shapes=[
            pltpu.VMEM((wide, wide), BF16),
            pltpu.VMEM((wide, wide), BF16),
            pltpu.VMEM((height // 2, 2 * wide), BF16),
        ],
        compiler_params=pltpu.CompilerParams(vmem_limit_bytes=40 * MIB),
        cost_estimate=pl.CostEstimate(
            flops=2 * groups * height * wide * 3 * height, bytes_accessed=8 * MIB, transcendentals=0
        ),
        name="column_filter",
    )(received, fwd, inv, spread, flat(w_first), b_first, flat(w_second), b_second)


def inverse_kernel(pitch, x_ref, table_ref, out_ref, turn_s, spec_s):
    owners, two_rows, wide = x_ref.shape[1:]
    rows = two_rows // 2
    channels = wide // 2
    parts, _, half = spec_s.shape
    chan_block = out_ref.shape[1]
    which = pl.program_id(0)
    step = pl.program_id(1)

    @pl.when(step == 0)
    def _():
        for r in range(2):
            for kk in range(2):
                for d in range(owners):
                    start = ((r * 2 + kk) * owners + d) * pitch
                    turn_s[start : start + rows, :] = x_ref[
                        which, d, r * rows : (r + 1) * rows, kk * channels : (kk + 1) * channels
                    ].astype(F32)
        for h in range(rows):
            for p in range(parts):
                turned = turn_s[pl.ds(p * half * pitch + h, half, stride=pitch), :].T
                spec_s[p, pl.ds(h, channels, stride=pitch), :] = turned

    spec = []
    for c in range(chan_block):
        start = pl.multiple_of(step * (chan_block * pitch), chan_block * pitch) + c * pitch
        spec.append(jnp.concatenate([spec_s[p, pl.ds(start, rows), :].astype(BF16) for p in range(parts)], axis=1))
    mixed = jnp.dot(jnp.concatenate(spec, axis=0), table_ref[...], preferred_element_type=F32)
    out_ref[0] = mixed.astype(BF16).reshape(chan_block, rows, -1)


def inverse_rows(received, table):
    slices, owners, two_rows, wide = received.shape
    rows = two_rows // 2
    channels = wide // 2
    two_k, width = table.shape
    chan_block = min(32, channels)
    pitch = rows + 8
    vmem = pl.BlockSpec(memory_space=pltpu.VMEM)
    return pl.pallas_call(
        functools.partial(inverse_kernel, pitch),
        grid=(slices, channels // chan_block),
        in_specs=[vmem, vmem],
        out_specs=pl.BlockSpec((1, chan_block, rows, width), lambda b, i: (b, i, 0, 0)),
        out_shape=jax.ShapeDtypeStruct((slices, channels, rows, width), BF16),
        scratch_shapes=[
            pltpu.VMEM((two_k * pitch, channels), F32),
            pltpu.VMEM((2, channels * pitch, two_k // 2), F32),
        ],
        compiler_params=pltpu.CompilerParams(vmem_limit_bytes=24 * MIB),
        cost_estimate=pl.CostEstimate(
            flops=2 * slices * channels * rows * width * two_k,
            bytes_accessed=2 * slices * channels * rows * width,
            transcendentals=0,
        ),
        name="inverse_row_dft",
    )(received, table)


def exchange(blocks):
    shape = blocks.shape
    flat = blocks.reshape((shape[0] * shape[1],) + shape[2:])
    flat = lax.all_to_all(flat, ("blk", "row"), split_axis=0, concat_axis=0, tiled=True)
    return flat.reshape(shape)


def local(field, gain, w_first, b_first, w_second, b_second):
    slices, channels, rows, width = field.shape
    owners = lax.axis_size("row")
    modes_x = 2 * owners
    height = owners * rows
    fwd, inv = height_tables(height)
    spread = jnp.asarray(np.tile(np.eye(BLOCK_CH), (1, channels // BLOCK_CH)), BF16)
    table = jnp.asarray(forward_table(width, modes_x))

    swap = [(0, 1), (1, 0)]
    own = [channel_stats(field, b) for b in range(slices)]
    other = [lax.ppermute(s, "blk", swap) for s in own]
    send = None
    for b in range(slices):
        send = forward_slice(field, b, gain, own[b], other[b], table, owners, send)
    columns = exchange(send)
    filtered = filter_columns(
        columns, jnp.asarray(fwd), jnp.asarray(inv), spread, w_first, b_first, w_second, b_second
    )
    colfield = exchange(filtered)
    return inverse_rows(colfield, jnp.asarray(inverse_table(width, modes_x)))


def solution(mesh):
    return jax.shard_map(
        local,
        mesh=mesh,
        in_specs=(P(None, "blk", "row", None), P("blk"), P(), P(), P(), P()),
        out_specs=P(None, "blk", "row", None),
        check_vma=False,
    )
```

```python
import functools
import math

import jax
import jax.numpy as jnp
import ml_dtypes
import numpy as np
from jax import lax
from jax.experimental import pallas as pl
from jax.experimental.pallas import tpu as pltpu
from jax.sharding import PartitionSpec as P

BLOCK_CH = 32
EPS = 1e-05
SHRINK = 0.01
LANES = 128
BF16 = jnp.bfloat16
F32 = jnp.float32
MIB = 1 << 20


def _angles(first, second, count):
    phase = np.mod(np.outer(first, second), count)
    return phase.astype(np.float32) * np.float32(2.0 * math.pi / count)


def _bf16(values):
    return np.asarray(values, np.float32).astype(ml_dtypes.bfloat16)


def mode_order(modes):
    return np.arange(modes).reshape(-1, 2).T.reshape(-1)


def forward_table(count, modes):
    t = _angles(np.arange(count), mode_order(modes), count)
    scale = np.float32(1.0 / math.sqrt(count))
    return _bf16(np.concatenate([np.cos(t) * scale, -np.sin(t) * scale], axis=1))


def inverse_table(count, modes):
    order = mode_order(modes)
    t = _angles(order, np.arange(count), count)
    weight = np.where(order == 0, 1.0, 2.0)[:, None].astype(np.float32)
    weight = weight * np.float32(1.0 / math.sqrt(count))
    return _bf16(np.concatenate([np.cos(t) * weight, -np.sin(t) * weight], axis=0))


def height_tables(height):
    quarter = height // 4
    s = _angles(np.arange(quarter + 1), np.arange(height), height)
    scale = np.float32(1.0 / math.sqrt(height))
    cosine, sine = np.cos(s) * scale, np.sin(s) * scale
    last = np.zeros((16, height), np.float32)
    last[0], last[1] = cosine[quarter], sine[quarter]
    forward = np.concatenate([cosine[:quarter], sine[:quarter], last], axis=0)
    inverse = np.concatenate([cosine[:quarter].T, sine[:quarter].T], axis=1)
    return _bf16(forward), _bf16(inverse)


def stats_kernel(which, x_ref, slice_ref, stat_ref, pivot_s, first_s, second_s, sems):
    channels, rows, width = slice_ref.shape
    chunks = sems.shape[0]
    chunk = channels // chunks
    wide = min(512, width)
    copies = []
    for i in range(chunks):
        part = pl.ds(i * chunk, chunk)
        copies.append(pltpu.make_async_copy(x_ref.at[which, part], slice_ref.at[part], sems.at[i]))
        copies[-1].start()
    for i in range(chunks):
        copies[i].wait()
        for lane in range(0, width, wide):
            here = slice(lane, lane + wide)
            if i == 0:
                pivot = jnp.zeros((rows, wide), F32)
                for c in range(chunk):
                    pivot = pivot + slice_ref[c, :, here].astype(F32)
                pivot = pivot * (1.0 / chunk)
                pivot_s[:, here] = pivot
                first = jnp.zeros((rows, wide), F32)
                second = jnp.zeros((rows, wide), F32)
            else:
                pivot, first, second = pivot_s[:, here], first_s[:, here], second_s[:, here]
            for c in range(i * chunk, (i + 1) * chunk):
                shifted = slice_ref[c, :, here].astype(F32) - pivot
                first = first + shifted
                second = second + shifted * shifted
            if i < chunks - 1:
                first_s[:, here], second_s[:, here] = first, second
            else:
                offset = first * (1.0 / channels)
                mean = pivot + offset
                high = mean.astype(BF16)
                stat_ref[0, :, here] = high
                stat_ref[1, :, here] = (mean - high.astype(F32)).astype(BF16)
                stat_ref[2, :, here] = jnp.maximum(second - first * offset, 0.0).astype(BF16)


def channel_stats(field, which):
    _, channels, rows, width = field.shape
    vmem = pl.BlockSpec(memory_space=pltpu.VMEM)
    return pl.pallas_call(
        functools.partial(stats_kernel, which),
        in_specs=[pl.BlockSpec(memory_space=pltpu.HBM)],
        out_specs=[vmem, vmem],
        out_shape=[
            jax.ShapeDtypeStruct((channels, rows, width), BF16),
            jax.ShapeDtypeStruct((3, rows, width), BF16),
        ],
        scratch_shapes=[
            pltpu.VMEM((rows, width), F32),
            pltpu.VMEM((rows, width), F32),
            pltpu.VMEM((rows, width), F32),
            pltpu.SemaphoreType.DMA((8,)),
        ],
        compiler_params=pltpu.CompilerParams(vmem_limit_bytes=16 * MIB),
        cost_estimate=pl.CostEstimate(
            flops=5 * channels * rows * width, bytes_accessed=2 * channels * rows * width, transcendentals=0
        ),
        name="channel_stats",
    )(pltpu.with_memory_space_constraint(field, pltpu.HBM))


def forward_kernel(which, chan_block, pitch, x_ref, gain_ref, own_ref, other_ref, table_ref, *rest):
    send_ref, spec_s, turn_s = rest[-3:]
    channels, rows, width = x_ref.shape
    parts, _, half = spec_s.shape
    owners = send_ref.shape[1]

    own_mean = own_ref[0].astype(F32) + own_ref[1].astype(F32)
    other_mean = other_ref[0].astype(F32) + other_ref[1].astype(F32)
    delta = own_mean - other_mean
    total = 2.0 * channels
    moment = own_ref[2].astype(F32) + other_ref[2].astype(F32) + delta * delta * (channels * 0.5)
    mean = (own_mean + other_mean) * 0.5
    scale = lax.rsqrt(moment * (1.0 / total) + EPS)

    for first in range(0, channels, chan_block):
        field = x_ref[first : first + chan_block].astype(F32)
        normed = ((field - mean[None]) * scale[None]).astype(BF16)
        spec = jnp.dot(normed.reshape(chan_block * rows, width), table_ref[...], preferred_element_type=F32)
        for c in range(chan_block):
            start = (first + c) * pitch
            for p in range(parts):
                spec_s[p, start : start + rows, :] = spec[c * rows : (c + 1) * rows, p * half : (p + 1) * half]

    for h in range(rows):
        for p in range(parts):
            turned = spec_s[p, pl.ds(h, channels, stride=pitch), :].T * gain_ref[...]
            turn_s[pl.ds(p * half * pitch + h, half, stride=pitch), :] = turned
    for r in range(2):
        for kk in range(2):
            for d in range(owners):
                start = ((r * 2 + kk) * owners + d) * pitch
                send_ref[which, d, r * rows : (r + 1) * rows, kk * channels : (kk + 1) * channels] = turn_s[
                    start : start + rows, :
                ].astype(BF16)


def forward_slice(field, which, slices, gain, own, other, table, owners, send):
    channels, rows, width = field.shape
    two_k = table.shape[1]
    chan_block = min(32, channels)
    pitch = rows + 8
    aliased = [] if send is None else [send]
    vmem = pl.BlockSpec(memory_space=pltpu.VMEM)
    return pl.pallas_call(
        functools.partial(forward_kernel, which, chan_block, pitch),
        in_specs=[vmem] * (5 + len(aliased)),
        out_specs=vmem,
        out_shape=jax.ShapeDtypeStruct((slices, owners, 2 * rows, 2 * channels), BF16),
        scratch_shapes=[
            pltpu.VMEM((2, channels * pitch, two_k // 2), F32),
            pltpu.VMEM((two_k * pitch, channels), F32),
        ],
        input_output_aliases={5: 0} if aliased else {},
        compiler_params=pltpu.CompilerParams(vmem_limit_bytes=24 * MIB),
        cost_estimate=pl.CostEstimate(
            flops=2 * channels * rows * width * two_k,
            bytes_accessed=2 * channels * rows * width,
            transcendentals=0,
        ),
        name="norm_and_row_dft",
    )(field, gain.reshape(1, channels), own, other, table, *aliased)


def block_diagonal(weights, spread, lanes):
    tiled = jnp.dot(weights, spread, preferred_element_type=F32)
    row = lax.broadcasted_iota(jnp.int32, (lanes, lanes), 0) // BLOCK_CH
    col = lax.broadcasted_iota(jnp.int32, (lanes, lanes), 1) // BLOCK_CH
    return jnp.where(row == col, tiled, 0.0)


def fill_weights(w_ref, group, spread, big, lanes):
    mine = slice(group * lanes, (group + 1) * lanes)
    real = block_diagonal(w_ref[0, mine, :], spread, lanes)
    imag = block_diagonal(w_ref[1, mine, :], spread, lanes)
    big[:lanes, :lanes] = real.astype(BF16)
    big[:lanes, lanes:] = imag.astype(BF16)
    big[lanes:, :lanes] = (-imag).astype(BF16)
    big[lanes:, lanes:] = real.astype(BF16)


def bias_row(b_ref, group, lanes):
    mine = slice(group * lanes, (group + 1) * lanes)
    return jnp.concatenate([b_ref[0:1, mine], b_ref[1:2, mine]], axis=1)


def filter_kernel(x_ref, fwd_ref, inv_ref, spread_ref, w1_ref, b1_ref, w2_ref, b2_ref, out_ref, big1, big2, packed):
    groups, owners, two_rows, wide = x_ref.shape
    rows = two_rows // 2
    lanes = wide // 2
    height = owners * rows
    quarter = height // 4
    top = lax.broadcasted_iota(jnp.int32, (quarter, lanes), 0) == 0
    turn = lax.broadcasted_iota(jnp.int32, (8, 1), 0) % 4
    norm = 1.0 / math.sqrt(height)
    last_cos = jnp.where(turn == 0, norm, jnp.where(turn == 2, -norm, 0.0))
    last_sin = jnp.where(turn == 1, norm, jnp.where(turn == 3, -norm, 0.0))
    for group in range(groups):
        fill_weights(w1_ref, group, spread_ref[...], big1, lanes)
        fill_weights(w2_ref, group, spread_ref[...], big2, lanes)
        bias1 = bias_row(b1_ref, group, lanes)
        bias2 = bias_row(b2_ref, group, lanes)
        real_in = x_ref[group, :, :rows, :].reshape(height, wide)
        imag_in = x_ref[group, :, rows:, :].reshape(height, wide)
        from_real = jnp.dot(fwd_ref[...], real_in, preferred_element_type=F32)
        from_imag = jnp.dot(fwd_ref[...], imag_in, preferred_element_type=F32)
        extra = []
        for kk in range(2):
            part = slice(kk * lanes, (kk + 1) * lanes)
            cos_re, sin_re = from_real[:quarter, part], from_real[quarter : 2 * quarter, part]
            cos_im, sin_im = from_imag[:quarter, part], from_imag[quarter : 2 * quarter, part]
            last_re = from_real[2 * quarter : 2 * quarter + 1, part] - from_imag[2 * quarter + 1 : 2 * quarter + 2, part]
            last_im = from_imag[2 * quarter : 2 * quarter + 1, part] + from_real[2 * quarter + 1 : 2 * quarter + 2, part]
            plus = jnp.concatenate([cos_re + sin_im, cos_im - sin_re], axis=1)
            minus = jnp.concatenate(
                [jnp.where(top, last_re, cos_re - sin_im), jnp.where(top, last_im, cos_im + sin_re)], axis=1
            )
            spectrum = jnp.concatenate([plus, minus], axis=0).astype(BF16)
            hidden = jnp.dot(spectrum, big1[...], preferred_element_type=F32) + bias1
            hidden = jnp.maximum(hidden, 0.0).astype(BF16)
            mixed = jnp.dot(hidden, big2[...], preferred_element_type=F32) + bias2
            kept = mixed - jnp.clip(mixed, -SHRINK, SHRINK)
            plus_re, plus_im = kept[:quarter, :lanes], kept[:quarter, lanes:]
            minus_re, minus_im = kept[quarter:, :lanes], kept[quarter:, lanes:]
            last_re, last_im = minus_re[0:1], minus_im[0:1]
            minus_re = jnp.where(top, 0.0, minus_re)
            minus_im = jnp.where(top, 0.0, minus_im)
            packed[:quarter, part] = (plus_re + minus_re).astype(BF16)
            packed[:quarter, wide + kk * lanes : wide + (kk + 1) * lanes] = (plus_im + minus_im).astype(BF16)
            packed[quarter:, part] = (minus_im - plus_im).astype(BF16)
            packed[quarter:, wide + kk * lanes : wide + (kk + 1) * lanes] = (plus_re - minus_re).astype(BF16)
            extra.append((last_cos * last_re + last_sin * last_im, last_cos * last_im - last_sin * last_re))
        column = jnp.dot(inv_ref[...], packed[...], preferred_element_type=F32)
        extra = jnp.concatenate([extra[0][0], extra[1][0], extra[0][1], extra[1][1]], axis=1)
        column = (column.reshape(height // 8, 8, 2 * wide) + extra[None]).astype(BF16)
        column = column.reshape(height, 2 * wide)
        out_ref[group, :, :rows, :] = column[:, :wide].reshape(owners, rows, wide)
        out_ref[group, :, rows:, :] = column[:, wide:].reshape(owners, rows, wide)


def filter_columns(received, fwd, inv, spread, w_first, b_first, w_second, b_second):
    groups, owners, two_rows, wide = received.shape
    height = owners * two_rows // 2
    vmem = pl.BlockSpec(memory_space=pltpu.VMEM)

    def flat(w):
        return w.reshape(2, -1, BLOCK_CH)

    return pl.pallas_call(
        filter_kernel,
        in_specs=[vmem] * 8,
        out_specs=vmem,
        out_shape=jax.ShapeDtypeStruct(received.shape, BF16),
        scratch_shapes=[
            pltpu.VMEM((wide, wide), BF16),
            pltpu.VMEM((wide, wide), BF16),
            pltpu.VMEM((height // 2, 2 * wide), BF16),
        ],
        compiler_params=pltpu.CompilerParams(vmem_limit_bytes=40 * MIB),
        cost_estimate=pl.CostEstimate(
            flops=2 * groups * height * wide * 3 * height, bytes_accessed=8 * MIB, transcendentals=0
        ),
        name="column_filter",
    )(received, fwd, inv, spread, flat(w_first), b_first, flat(w_second), b_second)


def inverse_kernel(chan_block, pitch, x_ref, table_ref, out_ref, turn_s, spec_s, done_s, sems):
    slices, owners, two_rows, wide = x_ref.shape
    rows = two_rows // 2
    channels = wide // 2
    parts, _, half = spec_s.shape
    copies = []
    for which in range(slices):
        for r in range(2):
            for kk in range(2):
                for d in range(owners):
                    start = ((r * 2 + kk) * owners + d) * pitch
                    turn_s[start : start + rows, :] = x_ref[
                        which, d, r * rows : (r + 1) * rows, kk * channels : (kk + 1) * channels
                    ].astype(F32)
        for h in range(rows):
            for p in range(parts):
                turned = turn_s[pl.ds(p * half * pitch + h, half, stride=pitch), :].T
                spec_s[p, pl.ds(h, channels, stride=pitch), :] = turned
        for first in range(0, channels, chan_block):
            spec = []
            for c in range(first, first + chan_block):
                start = c * pitch
                both = [spec_s[p, start : start + rows, :].astype(BF16) for p in range(parts)]
                spec.append(jnp.concatenate(both, axis=1))
            mixed = jnp.dot(jnp.concatenate(spec, axis=0), table_ref[...], preferred_element_type=F32)
            block = pl.ds(first, chan_block)
            done_s[which, block] = mixed.astype(BF16).reshape(chan_block, rows, -1)
            copies.append(
                pltpu.make_async_copy(done_s.at[which, block], out_ref.at[which, block], sems.at[len(copies)])
            )
            copies[-1].start()
    for copy in copies:
        copy.wait()


def inverse_rows(received, table):
    slices, owners, two_rows, wide = received.shape
    rows = two_rows // 2
    channels = wide // 2
    two_k, width = table.shape
    chan_block = min(16, channels)
    pitch = rows + 8
    vmem = pl.BlockSpec(memory_space=pltpu.VMEM)
    return pl.pallas_call(
        functools.partial(inverse_kernel, chan_block, pitch),
        in_specs=[vmem, vmem],
        out_specs=pl.BlockSpec(memory_space=pltpu.HBM),
        out_shape=jax.ShapeDtypeStruct((slices, channels, rows, width), BF16),
        scratch_shapes=[
            pltpu.VMEM((two_k * pitch, channels), F32),
            pltpu.VMEM((2, channels * pitch, two_k // 2), F32),
            pltpu.VMEM((slices, channels, rows, width), BF16),
            pltpu.SemaphoreType.DMA((slices * channels // chan_block,)),
        ],
        compiler_params=pltpu.CompilerParams(vmem_limit_bytes=40 * MIB),
        cost_estimate=pl.CostEstimate(
            flops=2 * slices * channels * rows * width * two_k,
            bytes_accessed=2 * slices * channels * rows * width,
            transcendentals=0,
        ),
        name="inverse_row_dft",
    )(received, table)


def exchange(blocks):
    shape = blocks.shape
    flat = blocks.reshape((shape[0] * shape[1],) + shape[2:])
    flat = lax.all_to_all(flat, ("blk", "row"), split_axis=0, concat_axis=0, tiled=True)
    return flat.reshape(shape)


def local(field, gain, w_first, b_first, w_second, b_second):
    slices, channels, rows, width = field.shape
    owners = lax.axis_size("row")
    modes_x = 2 * owners
    height = owners * rows
    fwd, inv = height_tables(height)
    spread = jnp.asarray(np.tile(np.eye(BLOCK_CH), (1, channels // BLOCK_CH)), BF16)
    table = jnp.asarray(forward_table(width, modes_x))

    swap = [(0, 1), (1, 0)]
    held, own = zip(*[channel_stats(field, b) for b in range(slices)])
    other = [lax.ppermute(s, "blk", swap) for s in own]
    send = None
    for b in range(slices):
        send = forward_slice(held[b], b, slices, gain, own[b], other[b], table, owners, send)
    columns = exchange(send)
    filtered = filter_columns(
        columns, jnp.asarray(fwd), jnp.asarray(inv), spread, w_first, b_first, w_second, b_second
    )
    colfield = exchange(filtered)
    return inverse_rows(colfield, jnp.asarray(inverse_table(width, modes_x)))


def solution(mesh):
    return jax.shard_map(
        local,
        mesh=mesh,
        in_specs=(P(None, "blk", "row", None), P("blk"), P(), P(), P(), P()),
        out_specs=P(None, "blk", "row", None),
        check_vma=False,
    )
```

```python
import functools
import math

import jax
import jax.numpy as jnp
import ml_dtypes
import numpy as np
from jax import lax
from jax.experimental import pallas as pl
from jax.experimental.pallas import tpu as pltpu
from jax.sharding import PartitionSpec as P

BLOCK_CH = 32
EPS = 1e-05
SHRINK = 0.01
LANES = 128
BF16 = jnp.bfloat16
F32 = jnp.float32
MIB = 1 << 20


def _angles(first, second, count):
    phase = np.mod(np.outer(first, second), count)
    return phase.astype(np.float32) * np.float32(2.0 * math.pi / count)


def _bf16(values):
    return np.asarray(values, np.float32).astype(ml_dtypes.bfloat16)


def mode_order(modes):
    return np.arange(modes).reshape(-1, 2).T.reshape(-1)


def forward_table(count, modes):
    t = _angles(np.arange(count), mode_order(modes), count)
    scale = np.float32(1.0 / math.sqrt(count))
    return _bf16(np.concatenate([np.cos(t) * scale, -np.sin(t) * scale], axis=1))


def inverse_table(count, modes):
    order = mode_order(modes)
    t = _angles(order, np.arange(count), count)
    weight = np.where(order == 0, 1.0, 2.0)[:, None].astype(np.float32)
    weight = weight * np.float32(1.0 / math.sqrt(count))
    return _bf16(np.concatenate([np.cos(t) * weight, -np.sin(t) * weight], axis=0))


def height_tables(height):
    quarter = height // 4
    s = _angles(np.arange(quarter + 1), np.arange(height), height)
    scale = np.float32(1.0 / math.sqrt(height))
    cosine, sine = np.cos(s) * scale, np.sin(s) * scale
    last = np.zeros((16, height), np.float32)
    last[0], last[1] = cosine[quarter], sine[quarter]
    forward = np.concatenate([cosine[:quarter], sine[:quarter], last], axis=0)
    inverse = np.concatenate([cosine[:quarter].T, sine[:quarter].T], axis=1)
    return _bf16(forward), _bf16(inverse)


def stats_kernel(which, x_ref, slice_ref, stat_ref, pivot_s, first_s, second_s, sems):
    channels, rows, width = slice_ref.shape
    chunks = sems.shape[0]
    chunk = channels // chunks
    wide = min(512, width)
    copies = []
    for i in range(chunks):
        part = pl.ds(i * chunk, chunk)
        copies.append(pltpu.make_async_copy(x_ref.at[which, part], slice_ref.at[part], sems.at[i]))
        copies[-1].start()
    for i in range(chunks):
        copies[i].wait()
        for lane in range(0, width, wide):
            here = slice(lane, lane + wide)
            if i == 0:
                pivot = jnp.zeros((rows, wide), F32)
                for c in range(chunk):
                    pivot = pivot + slice_ref[c, :, here].astype(F32)
                pivot = (pivot * (1.0 / chunk)).astype(BF16)
                pivot_s[:, here] = pivot
                first = jnp.zeros((rows, wide), F32)
                second = jnp.zeros((rows, wide), F32)
            else:
                pivot, first, second = pivot_s[:, here], first_s[:, here], second_s[:, here]
            for c in range(i * chunk, (i + 1) * chunk, 2):
                one = slice_ref[c, :, here] - pivot
                two = slice_ref[c + 1, :, here] - pivot
                first = first + (one + two).astype(F32)
                second = second + (one * one + two * two).astype(F32)
            if i < chunks - 1:
                first_s[:, here], second_s[:, here] = first, second
            else:
                offset = first * (1.0 / channels)
                mean = pivot.astype(F32) + offset
                high = mean.astype(BF16)
                stat_ref[0, :, here] = high
                stat_ref[1, :, here] = (mean - high.astype(F32)).astype(BF16)
                stat_ref[2, :, here] = jnp.maximum(second - first * offset, 0.0).astype(BF16)


def channel_stats(field, which):
    _, channels, rows, width = field.shape
    vmem = pl.BlockSpec(memory_space=pltpu.VMEM)
    return pl.pallas_call(
        functools.partial(stats_kernel, which),
        in_specs=[pl.BlockSpec(memory_space=pltpu.HBM)],
        out_specs=[vmem, vmem],
        out_shape=[
            jax.ShapeDtypeStruct((channels, rows, width), BF16),
            jax.ShapeDtypeStruct((3, rows, width), BF16),
        ],
        scratch_shapes=[
            pltpu.VMEM((rows, width), BF16),
            pltpu.VMEM((rows, width), F32),
            pltpu.VMEM((rows, width), F32),
            pltpu.SemaphoreType.DMA((8,)),
        ],
        compiler_params=pltpu.CompilerParams(vmem_limit_bytes=16 * MIB),
        cost_estimate=pl.CostEstimate(
            flops=5 * channels * rows * width, bytes_accessed=2 * channels * rows * width, transcendentals=0
        ),
        name="channel_stats",
    )(pltpu.with_memory_space_constraint(field, pltpu.HBM))


def forward_kernel(which, chan_block, pitch, x_ref, gain_ref, own_ref, other_ref, table_ref, *rest):
    send_ref, spec_s, turn_s = rest[-3:]
    channels, rows, width = x_ref.shape
    parts, _, half = spec_s.shape
    owners = send_ref.shape[1]

    own_mean = own_ref[0].astype(F32) + own_ref[1].astype(F32)
    other_mean = other_ref[0].astype(F32) + other_ref[1].astype(F32)
    delta = own_mean - other_mean
    total = 2.0 * channels
    moment = own_ref[2].astype(F32) + other_ref[2].astype(F32) + delta * delta * (channels * 0.5)
    mean = (own_mean + other_mean) * 0.5
    scale = lax.rsqrt(moment * (1.0 / total) + EPS)

    for first in range(0, channels, chan_block):
        field = x_ref[first : first + chan_block].astype(F32)
        normed = ((field - mean[None]) * scale[None]).astype(BF16)
        spec = jnp.dot(normed.reshape(chan_block * rows, width), table_ref[...], preferred_element_type=F32)
        for c in range(chan_block):
            start = (first + c) * pitch
            for p in range(parts):
                spec_s[p, start : start + rows, :] = spec[c * rows : (c + 1) * rows, p * half : (p + 1) * half]

    for h in range(rows):
        for p in range(parts):
            turned = spec_s[p, pl.ds(h, channels, stride=pitch), :].T * gain_ref[...]
            turn_s[pl.ds(p * half * pitch + h, half, stride=pitch), :] = turned
    for r in range(2):
        for kk in range(2):
            for d in range(owners):
                start = ((r * 2 + kk) * owners + d) * pitch
                send_ref[which, d, r * rows : (r + 1) * rows, kk * channels : (kk + 1) * channels] = turn_s[
                    start : start + rows, :
                ].astype(BF16)


def forward_slice(field, which, slices, gain, own, other, table, owners, send):
    channels, rows, width = field.shape
    two_k = table.shape[1]
    chan_block = min(32, channels)
    pitch = rows + 8
    aliased = [] if send is None else [send]
    vmem = pl.BlockSpec(memory_space=pltpu.VMEM)
    return pl.pallas_call(
        functools.partial(forward_kernel, which, chan_block, pitch),
        in_specs=[vmem] * (5 + len(aliased)),
        out_specs=vmem,
        out_shape=jax.ShapeDtypeStruct((slices, owners, 2 * rows, 2 * channels), BF16),
        scratch_shapes=[
            pltpu.VMEM((2, channels * pitch, two_k // 2), F32),
            pltpu.VMEM((two_k * pitch, channels), F32),
        ],
        input_output_aliases={5: 0} if aliased else {},
        compiler_params=pltpu.CompilerParams(vmem_limit_bytes=24 * MIB),
        cost_estimate=pl.CostEstimate(
            flops=2 * channels * rows * width * two_k,
            bytes_accessed=2 * channels * rows * width,
            transcendentals=0,
        ),
        name="norm_and_row_dft",
    )(field, gain.reshape(1, channels), own, other, table, *aliased)


def block_diagonal(weights, spread, lanes):
    tiled = jnp.dot(weights, spread, preferred_element_type=F32)
    row = lax.broadcasted_iota(jnp.int32, (lanes, lanes), 0) // BLOCK_CH
    col = lax.broadcasted_iota(jnp.int32, (lanes, lanes), 1) // BLOCK_CH
    return jnp.where(row == col, tiled, 0.0)


def fill_weights(w_ref, group, spread, big, lanes):
    mine = slice(group * lanes, (group + 1) * lanes)
    real = block_diagonal(w_ref[0, mine, :], spread, lanes)
    imag = block_diagonal(w_ref[1, mine, :], spread, lanes)
    big[:lanes, :lanes] = real.astype(BF16)
    big[:lanes, lanes:] = imag.astype(BF16)
    big[lanes:, :lanes] = (-imag).astype(BF16)
    big[lanes:, lanes:] = real.astype(BF16)


def bias_row(b_ref, group, lanes):
    mine = slice(group * lanes, (group + 1) * lanes)
    return jnp.concatenate([b_ref[0:1, mine], b_ref[1:2, mine]], axis=1)


def filter_kernel(x_ref, fwd_ref, inv_ref, spread_ref, w1_ref, b1_ref, w2_ref, b2_ref, out_ref, big1, big2, spec_s, packed):
    groups, owners, two_rows, wide = x_ref.shape
    rows = two_rows // 2
    lanes = wide // 2
    height = owners * rows
    quarter = height // 4
    top = lax.broadcasted_iota(jnp.int32, (quarter, lanes), 0) == 0
    turn = lax.broadcasted_iota(jnp.int32, (8, 1), 0) % 4
    norm = 1.0 / math.sqrt(height)
    last_cos = jnp.where(turn == 0, norm, jnp.where(turn == 2, -norm, 0.0))
    last_sin = jnp.where(turn == 1, norm, jnp.where(turn == 3, -norm, 0.0))
    real_part = lambda kk: slice(kk * lanes, (kk + 1) * lanes)
    imag_part = lambda kk: slice(wide + kk * lanes, wide + (kk + 1) * lanes)

    def transform(group):
        real_in = x_ref[group, :, :rows, :].reshape(height, wide)
        imag_in = x_ref[group, :, rows:, :].reshape(height, wide)
        from_real = jnp.dot(fwd_ref[...], real_in, preferred_element_type=F32)
        from_imag = jnp.dot(fwd_ref[...], imag_in, preferred_element_type=F32)
        last = slice(2 * quarter, 2 * quarter + 1)
        last_sine = slice(2 * quarter + 1, 2 * quarter + 2)
        for kk in range(2):
            part = real_part(kk)
            cos_re, sin_re = from_real[:quarter, part], from_real[quarter : 2 * quarter, part]
            cos_im, sin_im = from_imag[:quarter, part], from_imag[quarter : 2 * quarter, part]
            last_re = from_real[last, part] - from_imag[last_sine, part]
            last_im = from_imag[last, part] + from_real[last_sine, part]
            spec_s[group, kk, :quarter, :lanes] = (cos_re + sin_im).astype(BF16)
            spec_s[group, kk, :quarter, lanes:] = (cos_im - sin_re).astype(BF16)
            spec_s[group, kk, quarter:, :lanes] = jnp.where(top, last_re, cos_re - sin_im).astype(BF16)
            spec_s[group, kk, quarter:, lanes:] = jnp.where(top, last_im, cos_im + sin_re).astype(BF16)

    def mix(group):
        extra_re, extra_im = [], []
        for kk in range(2):
            hidden = jnp.dot(spec_s[group, kk], big1[group], preferred_element_type=F32) + bias_row(b1_ref, group, lanes)
            hidden = jnp.maximum(hidden, 0.0).astype(BF16)
            mixed = jnp.dot(hidden, big2[group], preferred_element_type=F32) + bias_row(b2_ref, group, lanes)
            kept = mixed - jnp.clip(mixed, -SHRINK, SHRINK)
            plus_re, plus_im = kept[:quarter, :lanes], kept[:quarter, lanes:]
            minus_re, minus_im = kept[quarter:, :lanes], kept[quarter:, lanes:]
            last_re, last_im = minus_re[0:1], minus_im[0:1]
            minus_re = jnp.where(top, 0.0, minus_re)
            minus_im = jnp.where(top, 0.0, minus_im)
            packed[group, :quarter, real_part(kk)] = (plus_re + minus_re).astype(BF16)
            packed[group, :quarter, imag_part(kk)] = (plus_im + minus_im).astype(BF16)
            packed[group, quarter:, real_part(kk)] = (minus_im - plus_im).astype(BF16)
            packed[group, quarter:, imag_part(kk)] = (plus_re - minus_re).astype(BF16)
            extra_re.append(last_cos * last_re + last_sin * last_im)
            extra_im.append(last_cos * last_im - last_sin * last_re)
        return jnp.concatenate(extra_re + extra_im, axis=1)

    def invert(group, extra):
        column = jnp.dot(inv_ref[...], packed[group], preferred_element_type=F32)
        column = (column.reshape(height // 8, 8, 2 * wide) + extra[None]).astype(BF16)
        column = column.reshape(height, 2 * wide)
        out_ref[group, :, :rows, :] = column[:, :wide].reshape(owners, rows, wide)
        out_ref[group, :, rows:, :] = column[:, wide:].reshape(owners, rows, wide)

    for group in range(groups):
        fill_weights(w1_ref, group, spread_ref[...], big1.at[group], lanes)
        fill_weights(w2_ref, group, spread_ref[...], big2.at[group], lanes)
    for group in range(groups):
        transform(group)
    extra = [mix(group) for group in range(groups)]
    for group in range(groups):
        invert(group, extra[group])


def filter_columns(received, fwd, inv, spread, w_first, b_first, w_second, b_second):
    groups, owners, two_rows, wide = received.shape
    height = owners * two_rows // 2
    vmem = pl.BlockSpec(memory_space=pltpu.VMEM)

    def flat(w):
        return w.reshape(2, -1, BLOCK_CH)

    return pl.pallas_call(
        filter_kernel,
        in_specs=[vmem] * 8,
        out_specs=vmem,
        out_shape=jax.ShapeDtypeStruct(received.shape, BF16),
        scratch_shapes=[
            pltpu.VMEM((groups, wide, wide), BF16),
            pltpu.VMEM((groups, wide, wide), BF16),
            pltpu.VMEM((groups, 2, height // 2, wide), BF16),
            pltpu.VMEM((groups, height // 2, 2 * wide), BF16),
        ],
        compiler_params=pltpu.CompilerParams(vmem_limit_bytes=40 * MIB),
        cost_estimate=pl.CostEstimate(
            flops=2 * groups * height * wide * 3 * height, bytes_accessed=8 * MIB, transcendentals=0
        ),
        name="column_filter",
    )(received, fwd, inv, spread, flat(w_first), b_first, flat(w_second), b_second)


def inverse_kernel(chan_block, pitch, x_ref, table_ref, out_ref, turn_s, spec_s, done_s, sems):
    slices, owners, two_rows, wide = x_ref.shape
    rows = two_rows // 2
    channels = wide // 2
    parts, _, half = spec_s.shape
    copies = []
    for which in range(slices):
        for r in range(2):
            for kk in range(2):
                for d in range(owners):
                    start = ((r * 2 + kk) * owners + d) * pitch
                    turn_s[start : start + rows, :] = x_ref[
                        which, d, r * rows : (r + 1) * rows, kk * channels : (kk + 1) * channels
                    ].astype(F32)
        for h in range(rows):
            for p in range(parts):
                turned = turn_s[pl.ds(p * half * pitch + h, half, stride=pitch), :].T
                spec_s[p, pl.ds(h, channels, stride=pitch), :] = turned
        for first in range(0, channels, chan_block):
            spec = []
            for c in range(first, first + chan_block):
                start = c * pitch
                both = [spec_s[p, start : start + rows, :].astype(BF16) for p in range(parts)]
                spec.append(jnp.concatenate(both, axis=1))
            mixed = jnp.dot(jnp.concatenate(spec, axis=0), table_ref[...], preferred_element_type=F32)
            block = pl.ds(first, chan_block)
            done_s[which, block] = mixed.astype(BF16).reshape(chan_block, rows, -1)
            copies.append(
                pltpu.make_async_copy(done_s.at[which, block], out_ref.at[which, block], sems.at[len(copies)])
            )
            copies[-1].start()
    for copy in copies:
        copy.wait()


def inverse_rows(received, table):
    slices, owners, two_rows, wide = received.shape
    rows = two_rows // 2
    channels = wide // 2
    two_k, width = table.shape
    chan_block = min(16, channels)
    pitch = rows + 8
    vmem = pl.BlockSpec(memory_space=pltpu.VMEM)
    return pl.pallas_call(
        functools.partial(inverse_kernel, chan_block, pitch),
        in_specs=[vmem, vmem],
        out_specs=pl.BlockSpec(memory_space=pltpu.HBM),
        out_shape=jax.ShapeDtypeStruct((slices, channels, rows, width), BF16),
        scratch_shapes=[
            pltpu.VMEM((two_k * pitch, channels), F32),
            pltpu.VMEM((2, channels * pitch, two_k // 2), F32),
            pltpu.VMEM((slices, channels, rows, width), BF16),
            pltpu.SemaphoreType.DMA((slices * channels // chan_block,)),
        ],
        compiler_params=pltpu.CompilerParams(vmem_limit_bytes=40 * MIB),
        cost_estimate=pl.CostEstimate(
            flops=2 * slices * channels * rows * width * two_k,
            bytes_accessed=2 * slices * channels * rows * width,
            transcendentals=0,
        ),
        name="inverse_row_dft",
    )(received, table)


def exchange(blocks):
    shape = blocks.shape
    flat = blocks.reshape((shape[0] * shape[1],) + shape[2:])
    flat = lax.all_to_all(flat, ("blk", "row"), split_axis=0, concat_axis=0, tiled=True)
    return flat.reshape(shape)


def local(field, gain, w_first, b_first, w_second, b_second):
    slices, channels, rows, width = field.shape
    owners = lax.axis_size("row")
    modes_x = 2 * owners
    height = owners * rows
    fwd, inv = height_tables(height)
    spread = jnp.asarray(np.tile(np.eye(BLOCK_CH), (1, channels // BLOCK_CH)), BF16)
    table = jnp.asarray(forward_table(width, modes_x))

    swap = [(0, 1), (1, 0)]
    held, own = zip(*[channel_stats(field, b) for b in range(slices)])
    other = [lax.ppermute(s, "blk", swap) for s in own]
    send = None
    for b in range(slices):
        send = forward_slice(held[b], b, slices, gain, own[b], other[b], table, owners, send)
    columns = exchange(send)
    filtered = filter_columns(
        columns, jnp.asarray(fwd), jnp.asarray(inv), spread, w_first, b_first, w_second, b_second
    )
    colfield = exchange(filtered)
    return inverse_rows(colfield, jnp.asarray(inverse_table(width, modes_x)))


def solution(mesh):
    return jax.shard_map(
        local,
        mesh=mesh,
        in_specs=(P(None, "blk", "row", None), P("blk"), P(), P(), P(), P()),
        out_specs=P(None, "blk", "row", None),
        check_vma=False,
    )
```

```python
import functools
import math

import jax
import jax.numpy as jnp
import ml_dtypes
import numpy as np
from jax import lax
from jax.experimental import pallas as pl
from jax.experimental.pallas import tpu as pltpu
from jax.sharding import PartitionSpec as P

BLOCK_CH = 32
EPS = 1e-05
SHRINK = 0.01
LANES = 128
BF16 = jnp.bfloat16
F32 = jnp.float32
MIB = 1 << 20


def _angles(first, second, count):
    phase = np.mod(np.outer(first, second), count)
    return phase.astype(np.float32) * np.float32(2.0 * math.pi / count)


def _bf16(values):
    return np.asarray(values, np.float32).astype(ml_dtypes.bfloat16)


def mode_order(modes):
    return np.arange(modes).reshape(-1, 2).T.reshape(-1)


def forward_table(count, modes):
    t = _angles(np.arange(count), mode_order(modes), count)
    scale = np.float32(1.0 / math.sqrt(count))
    return _bf16(np.concatenate([np.cos(t) * scale, -np.sin(t) * scale], axis=1))


def inverse_table(count, modes):
    order = mode_order(modes)
    t = _angles(order, np.arange(count), count)
    weight = np.where(order == 0, 1.0, 2.0)[:, None].astype(np.float32)
    weight = weight * np.float32(1.0 / math.sqrt(count))
    both = np.stack([np.cos(t) * weight, -np.sin(t) * weight])
    both = both.reshape(2, 2, modes // 2, count).transpose(1, 0, 2, 3)
    return _bf16(both.reshape(2 * modes, count))


def height_tables(height):
    quarter = height // 4
    s = _angles(np.arange(quarter + 1), np.arange(height), height)
    scale = np.float32(1.0 / math.sqrt(height))
    cosine, sine = np.cos(s) * scale, np.sin(s) * scale
    last = np.zeros((16, height), np.float32)
    last[0], last[1] = cosine[quarter], sine[quarter]
    forward = np.concatenate([cosine[:quarter], sine[:quarter], last], axis=0)
    inverse = np.concatenate([cosine[:quarter].T, sine[:quarter].T], axis=1)
    return _bf16(forward), _bf16(inverse)


STEP = 16


def copies_of(segments, x_ref, held_refs, sems):
    found = []
    taken = 0
    for (which, first, lanes), ref in zip(segments, held_refs):
        channels, _, width = x_ref.shape[1], x_ref.shape[2], x_ref.shape[3]
        size = STEP * max(1, width // lanes)
        copies = []
        for c in range(0, channels, size):
            part = pl.ds(c, size)
            source = x_ref.at[which, part, :, pl.ds(first, lanes)]
            copies.append(pltpu.make_async_copy(source, ref.at[part], sems.at[taken]))
            taken += 1
        found.append((copies, size))
    return found


def stats_kernel(segments, x_ref, *refs):
    held_refs = refs[: len(segments)]
    stat_ref, pivot_s, first_s, second_s, sems = refs[len(segments) :]
    channels = x_ref.shape[1]
    rows = x_ref.shape[2]
    segment_copies = copies_of(segments, x_ref, held_refs, sems)
    for copies, _ in segment_copies:
        for copy in copies:
            copy.start()
    base = 0
    for (_, _, lanes), ref, (copies, size) in zip(segments, held_refs, segment_copies):
        wide = 512 if lanes % 512 == 0 else min(256, lanes)
        for at in range(0, channels, STEP):
            if at % size == 0:
                copies[at // size].wait()
            for lane in range(0, lanes, wide):
                there = slice(lane, lane + wide)
                here = slice(base + lane, base + lane + wide)
                if at == 0:
                    pivot = jnp.zeros((rows, wide), F32)
                    for c in range(STEP):
                        pivot = pivot + ref[c, :, there].astype(F32)
                    pivot = (pivot * (1.0 / STEP)).astype(BF16)
                    pivot_s[:, here] = pivot
                    first = jnp.zeros((rows, wide), F32)
                    second = jnp.zeros((rows, wide), F32)
                else:
                    pivot, first, second = pivot_s[:, here], first_s[:, here], second_s[:, here]
                for c in range(at, at + STEP, 2):
                    one = ref[c, :, there] - pivot
                    two = ref[c + 1, :, there] - pivot
                    first = first + (one + two).astype(F32)
                    second = second + (one * one + two * two).astype(F32)
                if at + STEP < channels:
                    first_s[:, here], second_s[:, here] = first, second
                else:
                    offset = first * (1.0 / channels)
                    mean = pivot.astype(F32) + offset
                    high = mean.astype(BF16)
                    stat_ref[0, :, here] = high
                    stat_ref[1, :, here] = (mean - high.astype(F32)).astype(BF16)
                    stat_ref[2, :, here] = jnp.maximum(second - first * offset, 0.0).astype(BF16)
        base += lanes


def channel_stats(field, segments):
    _, channels, rows, width = field.shape
    total = sum(lanes for _, _, lanes in segments)
    count = sum(channels // (STEP * max(1, width // lanes)) for _, _, lanes in segments)
    vmem = pl.BlockSpec(memory_space=pltpu.VMEM)
    *held, stat = pl.pallas_call(
        functools.partial(stats_kernel, segments),
        in_specs=[pl.BlockSpec(memory_space=pltpu.HBM)],
        out_specs=[vmem] * (len(segments) + 1),
        out_shape=[jax.ShapeDtypeStruct((channels, rows, lanes), BF16) for _, _, lanes in segments]
        + [jax.ShapeDtypeStruct((3, rows, total), BF16)],
        scratch_shapes=[
            pltpu.VMEM((rows, total), BF16),
            pltpu.VMEM((rows, total), F32),
            pltpu.VMEM((rows, total), F32),
            pltpu.SemaphoreType.DMA((count,)),
        ],
        compiler_params=pltpu.CompilerParams(vmem_limit_bytes=16 * MIB),
        cost_estimate=pl.CostEstimate(
            flops=5 * channels * rows * total, bytes_accessed=2 * channels * rows * total, transcendentals=0
        ),
        name="channel_stats",
    )(pltpu.with_memory_space_constraint(field, pltpu.HBM))
    return held, stat


def normalizer(own_ref, other_ref, here, channels):
    own_mean = own_ref[0, :, here].astype(F32) + own_ref[1, :, here].astype(F32)
    other_mean = other_ref[0, :, here].astype(F32) + other_ref[1, :, here].astype(F32)
    delta = own_mean - other_mean
    moment = own_ref[2, :, here].astype(F32) + other_ref[2, :, here].astype(F32) + delta * delta * (channels * 0.5)
    return (own_mean + other_mean) * 0.5, lax.rsqrt(moment * (0.5 / channels) + EPS)


def project(x_ref, stats, table_ref, first_row, pitch, add_ref, spec_ref, chan_block=32):
    channels, rows, lanes = x_ref.shape
    parts, _, half = spec_ref.shape
    mean, scale = stats
    table = table_ref[first_row : first_row + lanes, :]
    for first in range(0, channels, chan_block):
        field = x_ref[first : first + chan_block].astype(F32)
        normed = ((field - mean[None]) * scale[None]).astype(BF16)
        spec = jnp.dot(normed.reshape(chan_block * rows, lanes), table, preferred_element_type=F32)
        for c in range(chan_block):
            start = (first + c) * pitch
            for p in range(parts):
                value = spec[c * rows : (c + 1) * rows, p * half : (p + 1) * half]
                if add_ref is not None:
                    value = value + add_ref[p, start : start + rows, :]
                spec_ref[p, start : start + rows, :] = value


def hand_out(which, gain_ref, spec_s, turn_s, send_ref, rows, pitch):
    parts, _, half = spec_s.shape
    channels = turn_s.shape[-1]
    owners = send_ref.shape[1]
    for h in range(rows):
        for p in range(parts):
            turned = spec_s[p, pl.ds(h, channels, stride=pitch), :].T * gain_ref[...]
            turn_s[pl.ds(p * half * pitch + h, half, stride=pitch), :] = turned
    for r in range(2):
        for kk in range(2):
            for d in range(owners):
                start = ((r * 2 + kk) * owners + d) * pitch
                send_ref[which, d, r * rows : (r + 1) * rows, kk * channels : (kk + 1) * channels] = turn_s[
                    start : start + rows, :
                ].astype(BF16)


def forward_first(pitch, x_ref, early_ref, gain_ref, own_ref, other_ref, table_ref, send_ref, part_ref, spec_s, turn_s):
    channels, rows, width = x_ref.shape
    cut = early_ref.shape[2]
    project(x_ref, normalizer(own_ref, other_ref, slice(0, width), channels), table_ref, 0, pitch, None, spec_s)
    hand_out(0, gain_ref, spec_s, turn_s, send_ref, rows, pitch)
    stats = normalizer(own_ref, other_ref, slice(width, width + cut), channels)
    project(early_ref, stats, table_ref, 0, pitch, None, part_ref)


def forward_second(pitch, x_ref, gain_ref, own_ref, other_ref, table_ref, part_ref, _, send_ref, spec_s, turn_s):
    channels, rows, lanes = x_ref.shape
    cut = table_ref.shape[0] - lanes
    stats = normalizer(own_ref, other_ref, slice(0, lanes), channels)
    project(x_ref, stats, table_ref, cut, pitch, part_ref, spec_s)
    hand_out(1, gain_ref, spec_s, turn_s, send_ref, rows, pitch)


def forward_rows(kernel, held, gain, own, other, table, owners, more=()):
    channels, rows, _ = held[0].shape
    width, two_k = table.shape
    pitch = rows + 8
    vmem = pl.BlockSpec(memory_space=pltpu.VMEM)
    send = jax.ShapeDtypeStruct((2, owners, 2 * rows, 2 * channels), BF16)
    part = jax.ShapeDtypeStruct((2, channels * pitch, two_k // 2), F32)
    lanes = sum(x.shape[2] for x in held)
    return pl.pallas_call(
        functools.partial(kernel, pitch),
        in_specs=[vmem] * (len(held) + 4 + len(more)),
        out_specs=vmem if more else [vmem, vmem],
        out_shape=send if more else [send, part],
        scratch_shapes=[
            pltpu.VMEM((2, channels * pitch, two_k // 2), F32),
            pltpu.VMEM((two_k * pitch, channels), F32),
        ],
        input_output_aliases={len(held) + 5: 0} if more else {},
        compiler_params=pltpu.CompilerParams(vmem_limit_bytes=24 * MIB),
        cost_estimate=pl.CostEstimate(
            flops=2 * channels * rows * lanes * two_k, bytes_accessed=2 * channels * rows * lanes, transcendentals=0
        ),
        name="norm_and_row_dft",
    )(*held, gain.reshape(1, channels), own, other, table, *more)


def block_diagonal(weights, spread, lanes):
    tiled = jnp.dot(weights, spread, preferred_element_type=F32)
    row = lax.broadcasted_iota(jnp.int32, (lanes, lanes), 0) // BLOCK_CH
    col = lax.broadcasted_iota(jnp.int32, (lanes, lanes), 1) // BLOCK_CH
    return jnp.where(row == col, tiled, 0.0)


def fill_weights(w_ref, group, spread, big, lanes, turned=None):
    mine = slice(group * lanes, (group + 1) * lanes)
    real = block_diagonal(w_ref[0, mine, :], spread, lanes)
    imag = block_diagonal(w_ref[1, mine, :], spread, lanes)
    for target, shift in ((big, 0), (turned, lanes // 2)):
        if target is not None:
            re = pltpu.roll(real, shift, 1) if shift else real
            im = pltpu.roll(imag, shift, 1) if shift else imag
            target[:lanes, :lanes] = re.astype(BF16)
            target[:lanes, lanes:] = im.astype(BF16)
            target[lanes:, :lanes] = (-im).astype(BF16)
            target[lanes:, lanes:] = re.astype(BF16)


def bias_row(b_ref, group, lanes, shift=0):
    mine = slice(group * lanes, (group + 1) * lanes)
    both = [b_ref[0:1, mine], b_ref[1:2, mine]]
    if shift:
        both = [pltpu.roll(b, shift, 1) for b in both]
    return jnp.concatenate(both, axis=1)


def filter_kernel(x_ref, fwd_ref, inv_ref, spread_ref, w1_ref, b1_ref, w2_ref, b2_ref, out_ref, big1, big2, big2_turned, spec_s, packed):
    groups, owners, two_rows, wide = x_ref.shape
    rows = two_rows // 2
    lanes = wide // 2
    height = owners * rows
    quarter = height // 4
    top = lax.broadcasted_iota(jnp.int32, (quarter, lanes), 0) == 0
    turn = lax.broadcasted_iota(jnp.int32, (8, 1), 0) % 4
    norm = 1.0 / math.sqrt(height)
    last_cos = jnp.where(turn == 0, norm, jnp.where(turn == 2, -norm, 0.0))
    last_sin = jnp.where(turn == 1, norm, jnp.where(turn == 3, -norm, 0.0))
    real_part = lambda kk: slice(kk * lanes, (kk + 1) * lanes)

    def transform(group):
        real_in = x_ref[group, :, :rows, :].reshape(height, wide)
        imag_in = x_ref[group, :, rows:, :].reshape(height, wide)
        from_real = jnp.dot(fwd_ref[...], real_in, preferred_element_type=F32)
        from_imag = jnp.dot(fwd_ref[...], imag_in, preferred_element_type=F32)
        last = slice(2 * quarter, 2 * quarter + 1)
        last_sine = slice(2 * quarter + 1, 2 * quarter + 2)
        for kk in range(2):
            part = real_part(kk)
            cos_re, sin_re = from_real[:quarter, part], from_real[quarter : 2 * quarter, part]
            cos_im, sin_im = from_imag[:quarter, part], from_imag[quarter : 2 * quarter, part]
            last_re = from_real[last, part] - from_imag[last_sine, part]
            last_im = from_imag[last, part] + from_real[last_sine, part]
            spec_s[group, kk, :quarter, :lanes] = (cos_re + sin_im).astype(BF16)
            spec_s[group, kk, :quarter, lanes:] = (cos_im - sin_re).astype(BF16)
            spec_s[group, kk, quarter:, :lanes] = jnp.where(top, last_re, cos_re - sin_im).astype(BF16)
            spec_s[group, kk, quarter:, lanes:] = jnp.where(top, last_im, cos_im + sin_re).astype(BF16)

    def mix(group):
        values, extras = [], []
        for kk in range(2):
            shift = kk * (lanes // 2)
            second = (big2 if kk == 0 else big2_turned)[group]
            hidden = jnp.dot(spec_s[group, kk], big1[group], preferred_element_type=F32) + bias_row(b1_ref, group, lanes)
            hidden = jnp.maximum(hidden, 0.0).astype(BF16)
            mixed = jnp.dot(hidden, second, preferred_element_type=F32) + bias_row(b2_ref, group, lanes, shift)
            kept = mixed - jnp.clip(mixed, -SHRINK, SHRINK)
            plus_re, plus_im = kept[:quarter, :lanes], kept[:quarter, lanes:]
            minus_re, minus_im = kept[quarter:, :lanes], kept[quarter:, lanes:]
            last_re, last_im = minus_re[0:1], minus_im[0:1]
            minus_re = jnp.where(top, 0.0, minus_re)
            minus_im = jnp.where(top, 0.0, minus_im)
            values.append([plus_re + minus_re, plus_im + minus_im, minus_im - plus_im, plus_re - minus_re])
            extras.append([last_cos * last_re + last_sin * last_im, last_cos * last_im - last_sin * last_re])

        def halves(zero, one):
            low = lax.broadcasted_iota(jnp.int32, zero.shape, 1) < lanes // 2
            return jnp.where(low, zero, one), jnp.where(low, one, zero)

        for i, (zero, one) in enumerate(zip(*values)):
            for half, value in enumerate(halves(zero, one)):
                start = (i % 2) * wide + half * lanes
                packed[group, (i // 2) * quarter : (i // 2 + 1) * quarter, start : start + lanes] = value.astype(BF16)
        return jnp.concatenate([part for zero, one in zip(*extras) for part in halves(zero, one)], axis=1)

    def invert(group, extra):
        column = jnp.dot(inv_ref[...], packed[group], preferred_element_type=F32)
        column = (column.reshape(height // 8, 8, 2 * wide) + extra[None]).astype(BF16)
        column = column.reshape(height, 2 * wide)
        out_ref[group, :, :rows, :] = column[:, :wide].reshape(owners, rows, wide)
        out_ref[group, :, rows:, :] = column[:, wide:].reshape(owners, rows, wide)

    for group in range(groups):
        fill_weights(w1_ref, group, spread_ref[...], big1.at[group], lanes)
        fill_weights(w2_ref, group, spread_ref[...], big2.at[group], lanes, big2_turned.at[group])
    for group in range(groups):
        transform(group)
    extra = [mix(group) for group in range(groups)]
    for group in range(groups):
        invert(group, extra[group])


def filter_columns(received, fwd, inv, spread, w_first, b_first, w_second, b_second):
    groups, owners, two_rows, wide = received.shape
    height = owners * two_rows // 2
    vmem = pl.BlockSpec(memory_space=pltpu.VMEM)

    def flat(w):
        return w.reshape(2, -1, BLOCK_CH)

    return pl.pallas_call(
        filter_kernel,
        in_specs=[vmem] * 8,
        out_specs=vmem,
        out_shape=jax.ShapeDtypeStruct(received.shape, BF16),
        scratch_shapes=[
            pltpu.VMEM((groups, wide, wide), BF16),
            pltpu.VMEM((groups, wide, wide), BF16),
            pltpu.VMEM((groups, wide, wide), BF16),
            pltpu.VMEM((groups, 2, height // 2, wide), BF16),
            pltpu.VMEM((groups, height // 2, 2 * wide), BF16),
        ],
        compiler_params=pltpu.CompilerParams(vmem_limit_bytes=40 * MIB),
        cost_estimate=pl.CostEstimate(
            flops=2 * groups * height * wide * 3 * height, bytes_accessed=8 * MIB, transcendentals=0
        ),
        name="column_filter",
    )(received, fwd, inv, spread, flat(w_first), b_first, flat(w_second), b_second)


def inverse_kernel(chan_block, pitch, x_ref, table_ref, out_ref, turn_s, spec_s, done_s, sems):
    slices, owners, two_rows, wide = x_ref.shape
    rows = two_rows // 2
    lanes = wide // 2
    part = lanes // 2
    copies = []
    for which in range(slices):
        for half in range(2):
            for r in range(2):
                for d in range(owners):
                    start = (r * owners + d) * pitch
                    turn_s[half, start : start + rows, :] = x_ref[
                        which, d, r * rows : (r + 1) * rows, half * lanes : (half + 1) * lanes
                    ].astype(F32)
            for h in range(rows):
                turned = turn_s[half, pl.ds(h, 2 * owners, stride=pitch), :].T
                for place in range(2):
                    kk = place if half == 0 else 1 - place
                    spec_s[kk, pl.ds(half * part * pitch + h, part, stride=pitch), :] = turned[
                        place * part : (place + 1) * part
                    ]
            for first in range(half * part, (half + 1) * part, chan_block):
                spec = []
                for c in range(first, first + chan_block):
                    start = c * pitch
                    both = [spec_s[kk, start : start + rows, :].astype(BF16) for kk in range(2)]
                    spec.append(jnp.concatenate(both, axis=1))
                mixed = jnp.dot(jnp.concatenate(spec, axis=0), table_ref[...], preferred_element_type=F32)
                block = pl.ds(first, chan_block)
                done_s[which, block] = mixed.astype(BF16).reshape(chan_block, rows, -1)
                copies.append(
                    pltpu.make_async_copy(done_s.at[which, block], out_ref.at[which, block], sems.at[len(copies)])
                )
                copies[-1].start()
    for copy in copies:
        copy.wait()


def inverse_rows(received, table):
    slices, owners, two_rows, wide = received.shape
    rows = two_rows // 2
    channels = wide // 2
    two_k, width = table.shape
    chan_block = min(16, channels)
    pitch = rows + 8
    vmem = pl.BlockSpec(memory_space=pltpu.VMEM)
    return pl.pallas_call(
        functools.partial(inverse_kernel, chan_block, pitch),
        in_specs=[vmem, vmem],
        out_specs=pl.BlockSpec(memory_space=pltpu.HBM),
        out_shape=jax.ShapeDtypeStruct((slices, channels, rows, width), BF16),
        scratch_shapes=[
            pltpu.VMEM((2, two_k // 2 * pitch, channels), F32),
            pltpu.VMEM((2, channels * pitch, two_k // 2), F32),
            pltpu.VMEM((slices, channels, rows, width), BF16),
            pltpu.SemaphoreType.DMA((slices * channels // chan_block,)),
        ],
        compiler_params=pltpu.CompilerParams(vmem_limit_bytes=40 * MIB),
        cost_estimate=pl.CostEstimate(
            flops=2 * slices * channels * rows * width * two_k,
            bytes_accessed=2 * slices * channels * rows * width,
            transcendentals=0,
        ),
        name="inverse_row_dft",
    )(received, table)


def exchange(blocks):
    shape = blocks.shape
    flat = blocks.reshape((shape[0] * shape[1],) + shape[2:])
    flat = lax.all_to_all(flat, ("blk", "row"), split_axis=0, concat_axis=0, tiled=True)
    return flat.reshape(shape)


def local(field, gain, w_first, b_first, w_second, b_second):
    slices, channels, rows, width = field.shape
    owners = lax.axis_size("row")
    modes_x = 2 * owners
    height = owners * rows
    fwd, inv = height_tables(height)
    spread = jnp.asarray(np.tile(np.eye(BLOCK_CH), (1, channels // BLOCK_CH)), BF16)
    table = jnp.asarray(forward_table(width, modes_x))

    swap = [(0, 1), (1, 0)]
    cut = width // 4
    groups = (((0, 0, width), (1, 0, cut)), ((1, cut, width - cut),))
    (held_first, own_first), (held_second, own_second) = [channel_stats(field, group) for group in groups]
    other_first = lax.ppermute(own_first, "blk", swap)
    other_second = lax.ppermute(own_second, "blk", swap)
    send, part = forward_rows(forward_first, held_first, gain, own_first, other_first, table, owners)
    send = forward_rows(
        forward_second, held_second, gain, own_second, other_second, table, owners, (part, send)
    )
    columns = exchange(send)
    filtered = filter_columns(
        columns, jnp.asarray(fwd), jnp.asarray(inv), spread, w_first, b_first, w_second, b_second
    )
    colfield = exchange(filtered)
    return inverse_rows(colfield, jnp.asarray(inverse_table(width, modes_x)))


def solution(mesh):
    return jax.shard_map(
        local,
        mesh=mesh,
        in_specs=(P(None, "blk", "row", None), P("blk"), P(), P(), P(), P()),
        out_specs=P(None, "blk", "row", None),
        check_vma=False,
    )
```

```python
import functools
import math

import jax
import jax.numpy as jnp
import ml_dtypes
import numpy as np
from jax import lax
from jax.experimental import pallas as pl
from jax.experimental.pallas import tpu as pltpu
from jax.sharding import PartitionSpec as P

BLOCK_CH = 32
EPS = 1e-05
SHRINK = 0.01
BF16 = jnp.bfloat16
F32 = jnp.float32
MIB = 1 << 20


def _angles(first, second, count):
    phase = np.mod(np.outer(first, second), count)
    return phase.astype(np.float32) * np.float32(2.0 * math.pi / count)


def _bf16(values):
    return np.asarray(values, np.float32).astype(ml_dtypes.bfloat16)


def mode_order(modes):
    return np.arange(modes).reshape(-1, 2).T.reshape(-1)


def forward_table(count, modes):
    t = _angles(np.arange(count), mode_order(modes), count)
    scale = np.float32(1.0 / math.sqrt(count))
    return _bf16(np.concatenate([np.cos(t) * scale, -np.sin(t) * scale], axis=1))


def inverse_table(count, modes):
    order = mode_order(modes)
    t = _angles(order, np.arange(count), count)
    weight = np.where(order == 0, 1.0, 2.0)[:, None].astype(np.float32)
    weight = weight * np.float32(1.0 / math.sqrt(count))
    both = np.stack([np.cos(t) * weight, -np.sin(t) * weight])
    both = both.reshape(2, 2, modes // 2, count).transpose(1, 0, 2, 3)
    return _bf16(both.reshape(2 * modes, count))


def height_tables(height):
    quarter = height // 4
    s = _angles(np.arange(quarter + 1), np.arange(height), height)
    scale = np.float32(1.0 / math.sqrt(height))
    cosine, sine = np.cos(s) * scale, np.sin(s) * scale
    last = np.zeros((16, height), np.float32)
    last[0], last[1] = cosine[quarter], sine[quarter]
    forward = np.concatenate([cosine[:quarter], sine[:quarter], last], axis=0)
    inverse = np.concatenate([cosine[:quarter].T, sine[:quarter].T], axis=1)
    return _bf16(forward), _bf16(inverse)


STEP = 16


def copies_of(segments, x_ref, held_refs, sems):
    found = []
    taken = 0
    for (which, first, lanes), ref in zip(segments, held_refs):
        channels, _, width = x_ref.shape[1], x_ref.shape[2], x_ref.shape[3]
        size = STEP * max(1, width // lanes)
        copies = []
        for c in range(0, channels, size):
            part = pl.ds(c, size)
            source = x_ref.at[which, part, :, pl.ds(first, lanes)]
            copies.append(pltpu.make_async_copy(source, ref.at[part], sems.at[taken]))
            taken += 1
        found.append((copies, size))
    return found


def stats_kernel(segments, x_ref, *refs):
    held_refs = refs[: len(segments)]
    stat_ref, pivot_s, first_s, second_s, sems = refs[len(segments) :]
    channels = x_ref.shape[1]
    rows = x_ref.shape[2]
    segment_copies = copies_of(segments, x_ref, held_refs, sems)
    for copies, _ in segment_copies:
        for copy in copies:
            copy.start()
    base = 0
    for (_, _, lanes), ref, (copies, size) in zip(segments, held_refs, segment_copies):
        wide = 512 if lanes % 512 == 0 else min(256, lanes)
        for at in range(0, channels, STEP):
            if at % size == 0:
                copies[at // size].wait()
            for lane in range(0, lanes, wide):
                there = slice(lane, lane + wide)
                here = slice(base + lane, base + lane + wide)
                if at == 0:
                    pivot = jnp.zeros((rows, wide), F32)
                    for c in range(STEP):
                        pivot = pivot + ref[c, :, there].astype(F32)
                    pivot = (pivot * (1.0 / STEP)).astype(BF16)
                    pivot_s[:, here] = pivot
                    first = jnp.zeros((rows, wide), F32)
                    second = jnp.zeros((rows, wide), F32)
                else:
                    pivot, first, second = pivot_s[:, here], first_s[:, here], second_s[:, here]
                for c in range(at, at + STEP, 2):
                    one = ref[c, :, there] - pivot
                    two = ref[c + 1, :, there] - pivot
                    first = first + (one + two).astype(F32)
                    second = second + (one * one + two * two).astype(F32)
                if at + STEP < channels:
                    first_s[:, here], second_s[:, here] = first, second
                else:
                    offset = first * (1.0 / channels)
                    mean = pivot.astype(F32) + offset
                    high = mean.astype(BF16)
                    stat_ref[0, :, here] = high
                    stat_ref[1, :, here] = (mean - high.astype(F32)).astype(BF16)
                    stat_ref[2, :, here] = jnp.maximum(second - first * offset, 0.0).astype(BF16)
        base += lanes


def channel_stats(field, segments):
    _, channels, rows, width = field.shape
    total = sum(lanes for _, _, lanes in segments)
    count = sum(channels // (STEP * max(1, width // lanes)) for _, _, lanes in segments)
    vmem = pl.BlockSpec(memory_space=pltpu.VMEM)
    *held, stat = pl.pallas_call(
        functools.partial(stats_kernel, segments),
        in_specs=[pl.BlockSpec(memory_space=pltpu.HBM)],
        out_specs=[vmem] * (len(segments) + 1),
        out_shape=[jax.ShapeDtypeStruct((channels, rows, lanes), BF16) for _, _, lanes in segments]
        + [jax.ShapeDtypeStruct((3, rows, total), BF16)],
        scratch_shapes=[
            pltpu.VMEM((rows, total), BF16),
            pltpu.VMEM((rows, total), F32),
            pltpu.VMEM((rows, total), F32),
            pltpu.SemaphoreType.DMA((count,)),
        ],
        compiler_params=pltpu.CompilerParams(vmem_limit_bytes=16 * MIB),
        cost_estimate=pl.CostEstimate(
            flops=5 * channels * rows * total, bytes_accessed=2 * channels * rows * total, transcendentals=0
        ),
        name="channel_stats",
    )(pltpu.with_memory_space_constraint(field, pltpu.HBM))
    return held, stat


def normalizer(own_ref, other_ref, here, channels):
    own_mean = own_ref[0, :, here].astype(F32) + own_ref[1, :, here].astype(F32)
    other_mean = other_ref[0, :, here].astype(F32) + other_ref[1, :, here].astype(F32)
    delta = own_mean - other_mean
    moment = own_ref[2, :, here].astype(F32) + other_ref[2, :, here].astype(F32) + delta * delta * (channels * 0.5)
    return (own_mean + other_mean) * 0.5, lax.rsqrt(moment * (0.5 / channels) + EPS)


def project(x_ref, stats, table_ref, first_row, pitch, add_ref, spec_ref, chan_block=32):
    channels, rows, lanes = x_ref.shape
    parts, _, half = spec_ref.shape
    mean, scale = stats
    table = table_ref[first_row : first_row + lanes, :]
    for first in range(0, channels, chan_block):
        field = x_ref[first : first + chan_block].astype(F32)
        normed = ((field - mean[None]) * scale[None]).astype(BF16)
        spec = jnp.dot(normed.reshape(chan_block * rows, lanes), table, preferred_element_type=F32)
        for c in range(chan_block):
            start = (first + c) * pitch
            for p in range(parts):
                value = spec[c * rows : (c + 1) * rows, p * half : (p + 1) * half]
                if add_ref is not None:
                    value = value + add_ref[p, start : start + rows, :]
                spec_ref[p, start : start + rows, :] = value
        yield


def hand_out(which, gain_ref, spec_s, turn_s, send_ref, rows, pitch, beside=()):
    parts, _, half = spec_s.shape
    channels = turn_s.shape[-1]
    owners = send_ref.shape[1]
    beside = iter(beside)
    for h in range(rows):
        if h % 4 == 0:
            next(beside, None)
        for p in range(parts):
            turned = spec_s[p, pl.ds(h, channels, stride=pitch), :].T * gain_ref[...]
            turn_s[pl.ds(p * half * pitch + h, half, stride=pitch), :] = turned
    for _ in beside:
        pass
    for r in range(2):
        for kk in range(2):
            for d in range(owners):
                start = ((r * 2 + kk) * owners + d) * pitch
                send_ref[which, d, r * rows : (r + 1) * rows, kk * channels : (kk + 1) * channels] = turn_s[
                    start : start + rows, :
                ].astype(BF16)


def forward_first(pitch, x_ref, early_ref, gain_ref, own_ref, other_ref, table_ref, send_ref, part_ref, spec_s, turn_s):
    channels, rows, width = x_ref.shape
    cut = early_ref.shape[2]
    stats = normalizer(own_ref, other_ref, slice(0, width), channels)
    for _ in project(x_ref, stats, table_ref, 0, pitch, None, spec_s):
        pass
    stats = normalizer(own_ref, other_ref, slice(width, width + cut), channels)
    early = project(early_ref, stats, table_ref, 0, pitch, None, part_ref)
    hand_out(0, gain_ref, spec_s, turn_s, send_ref, rows, pitch, early)


def forward_second(pitch, x_ref, gain_ref, own_ref, other_ref, table_ref, part_ref, _, send_ref, spec_s, turn_s):
    channels, rows, lanes = x_ref.shape
    cut = table_ref.shape[0] - lanes
    stats = normalizer(own_ref, other_ref, slice(0, lanes), channels)
    for _ in project(x_ref, stats, table_ref, cut, pitch, part_ref, spec_s):
        pass
    hand_out(1, gain_ref, spec_s, turn_s, send_ref, rows, pitch)


def forward_rows(kernel, held, gain, own, other, table, owners, more=()):
    channels, rows, _ = held[0].shape
    width, two_k = table.shape
    pitch = rows + 8
    vmem = pl.BlockSpec(memory_space=pltpu.VMEM)
    send = jax.ShapeDtypeStruct((2, owners, 2 * rows, 2 * channels), BF16)
    part = jax.ShapeDtypeStruct((2, (channels + 1) * pitch, two_k // 2), F32)
    lanes = sum(x.shape[2] for x in held)
    return pl.pallas_call(
        functools.partial(kernel, pitch),
        in_specs=[vmem] * (len(held) + 4 + len(more)),
        out_specs=vmem if more else [vmem, vmem],
        out_shape=send if more else [send, part],
        scratch_shapes=[
            pltpu.VMEM((2, (channels + 1) * pitch, two_k // 2), F32),
            pltpu.VMEM(((two_k + 1) * pitch, channels), F32),
        ],
        input_output_aliases={len(held) + 5: 0} if more else {},
        compiler_params=pltpu.CompilerParams(vmem_limit_bytes=24 * MIB),
        cost_estimate=pl.CostEstimate(
            flops=2 * channels * rows * lanes * two_k, bytes_accessed=2 * channels * rows * lanes, transcendentals=0
        ),
        name="norm_and_row_dft",
    )(*held, gain.reshape(1, channels), own, other, table, *more)


def block_diagonal(weights, spread, lanes):
    tiled = jnp.dot(weights, spread, preferred_element_type=F32)
    row = lax.broadcasted_iota(jnp.int32, (lanes, lanes), 0) // BLOCK_CH
    col = lax.broadcasted_iota(jnp.int32, (lanes, lanes), 1) // BLOCK_CH
    return jnp.where(row == col, tiled, 0.0)


def fill_weights(w_ref, group, spread, big, lanes, turned=None):
    mine = slice(group * lanes, (group + 1) * lanes)
    real = block_diagonal(w_ref[0, mine, :], spread, lanes)
    imag = block_diagonal(w_ref[1, mine, :], spread, lanes)
    for target, shift in ((big, 0), (turned, lanes // 2)):
        if target is not None:
            re = pltpu.roll(real, shift, 1) if shift else real
            im = pltpu.roll(imag, shift, 1) if shift else imag
            target[:lanes, :lanes] = re.astype(BF16)
            target[:lanes, lanes:] = im.astype(BF16)
            target[lanes:, :lanes] = (-im).astype(BF16)
            target[lanes:, lanes:] = re.astype(BF16)


def bias_row(b_ref, group, lanes, shift=0):
    mine = slice(group * lanes, (group + 1) * lanes)
    both = [b_ref[0:1, mine], b_ref[1:2, mine]]
    if shift:
        both = [pltpu.roll(b, shift, 1) for b in both]
    return jnp.concatenate(both, axis=1)


def filter_kernel(x_ref, fwd_ref, inv_ref, spread_ref, w1_ref, b1_ref, w2_ref, b2_ref, out_ref, big1, big2, big2_turned, spec_s, packed):
    groups, owners, two_rows, wide = x_ref.shape
    rows = two_rows // 2
    lanes = wide // 2
    height = owners * rows
    quarter = height // 4
    top = lax.broadcasted_iota(jnp.int32, (quarter, lanes), 0) == 0
    turn = lax.broadcasted_iota(jnp.int32, (8, 1), 0) % 4
    norm = 1.0 / math.sqrt(height)
    last_cos = jnp.where(turn == 0, norm, jnp.where(turn == 2, -norm, 0.0))
    last_sin = jnp.where(turn == 1, norm, jnp.where(turn == 3, -norm, 0.0))
    real_part = lambda kk: slice(kk * lanes, (kk + 1) * lanes)

    def transform(group):
        real_in = x_ref[group, :, :rows, :].reshape(height, wide)
        imag_in = x_ref[group, :, rows:, :].reshape(height, wide)
        from_real = jnp.dot(fwd_ref[...], real_in, preferred_element_type=F32)
        from_imag = jnp.dot(fwd_ref[...], imag_in, preferred_element_type=F32)
        last = slice(2 * quarter, 2 * quarter + 1)
        last_sine = slice(2 * quarter + 1, 2 * quarter + 2)
        for kk in range(2):
            part = real_part(kk)
            cos_re, sin_re = from_real[:quarter, part], from_real[quarter : 2 * quarter, part]
            cos_im, sin_im = from_imag[:quarter, part], from_imag[quarter : 2 * quarter, part]
            last_re = from_real[last, part] - from_imag[last_sine, part]
            last_im = from_imag[last, part] + from_real[last_sine, part]
            spec_s[group, kk, :quarter, :lanes] = (cos_re + sin_im).astype(BF16)
            spec_s[group, kk, :quarter, lanes:] = (cos_im - sin_re).astype(BF16)
            spec_s[group, kk, quarter:, :lanes] = jnp.where(top, last_re, cos_re - sin_im).astype(BF16)
            spec_s[group, kk, quarter:, lanes:] = jnp.where(top, last_im, cos_im + sin_re).astype(BF16)

    def mix(group):
        values, extras = [], []
        for kk in range(2):
            shift = kk * (lanes // 2)
            second = (big2 if kk == 0 else big2_turned)[group]
            hidden = jnp.dot(spec_s[group, kk], big1[group], preferred_element_type=F32) + bias_row(b1_ref, group, lanes)
            hidden = jnp.maximum(hidden, 0.0).astype(BF16)
            mixed = jnp.dot(hidden, second, preferred_element_type=F32) + bias_row(b2_ref, group, lanes, shift)
            kept = mixed - jnp.clip(mixed, -SHRINK, SHRINK)
            plus_re, plus_im = kept[:quarter, :lanes], kept[:quarter, lanes:]
            minus_re, minus_im = kept[quarter:, :lanes], kept[quarter:, lanes:]
            last_re, last_im = minus_re[0:1], minus_im[0:1]
            minus_re = jnp.where(top, 0.0, minus_re)
            minus_im = jnp.where(top, 0.0, minus_im)
            values.append([plus_re + minus_re, plus_im + minus_im, minus_im - plus_im, plus_re - minus_re])
            extras.append([last_cos * last_re + last_sin * last_im, last_cos * last_im - last_sin * last_re])

        def halves(zero, one):
            low = lax.broadcasted_iota(jnp.int32, zero.shape, 1) < lanes // 2
            return jnp.where(low, zero, one), jnp.where(low, one, zero)

        for i, (zero, one) in enumerate(zip(*values)):
            for half, value in enumerate(halves(zero, one)):
                start = (i % 2) * wide + half * lanes
                packed[group, (i // 2) * quarter : (i // 2 + 1) * quarter, start : start + lanes] = value.astype(BF16)
        return jnp.concatenate([part for zero, one in zip(*extras) for part in halves(zero, one)], axis=1)

    def invert(group, extra):
        column = jnp.dot(inv_ref[...], packed[group], preferred_element_type=F32)
        column = (column.reshape(height // 8, 8, 2 * wide) + extra[None]).astype(BF16)
        column = column.reshape(height, 2 * wide)
        out_ref[group, :, :rows, :] = column[:, :wide].reshape(owners, rows, wide)
        out_ref[group, :, rows:, :] = column[:, wide:].reshape(owners, rows, wide)

    for group in range(groups):
        fill_weights(w1_ref, group, spread_ref[...], big1.at[group], lanes)
        fill_weights(w2_ref, group, spread_ref[...], big2.at[group], lanes, big2_turned.at[group])
    for group in range(groups):
        transform(group)
    extra = [mix(group) for group in range(groups)]
    for group in range(groups):
        invert(group, extra[group])


def filter_columns(received, fwd, inv, spread, w_first, b_first, w_second, b_second):
    groups, owners, two_rows, wide = received.shape
    height = owners * two_rows // 2
    vmem = pl.BlockSpec(memory_space=pltpu.VMEM)

    def flat(w):
        return w.reshape(2, -1, BLOCK_CH)

    return pl.pallas_call(
        filter_kernel,
        in_specs=[vmem] * 8,
        out_specs=vmem,
        out_shape=jax.ShapeDtypeStruct(received.shape, BF16),
        scratch_shapes=[
            pltpu.VMEM((groups, wide, wide), BF16),
            pltpu.VMEM((groups, wide, wide), BF16),
            pltpu.VMEM((groups, wide, wide), BF16),
            pltpu.VMEM((groups, 2, height // 2, wide), BF16),
            pltpu.VMEM((groups, height // 2, 2 * wide), BF16),
        ],
        compiler_params=pltpu.CompilerParams(vmem_limit_bytes=40 * MIB),
        cost_estimate=pl.CostEstimate(
            flops=2 * groups * height * wide * 3 * height, bytes_accessed=8 * MIB, transcendentals=0
        ),
        name="column_filter",
    )(received, fwd, inv, spread, flat(w_first), b_first, flat(w_second), b_second)


def inverse_kernel(chan_block, pitch, x_ref, table_ref, out_ref, turn_s, spec_s, done_s, sems):
    slices, owners, two_rows, wide = x_ref.shape
    rows = two_rows // 2
    lanes = wide // 2
    part = lanes // 2
    copies = []
    for which in range(slices):
        for half in range(2):
            for r in range(2):
                for d in range(owners):
                    start = (r * owners + d) * pitch
                    turn_s[half, start : start + rows, :] = x_ref[
                        which, d, r * rows : (r + 1) * rows, half * lanes : (half + 1) * lanes
                    ].astype(F32)
            for h in range(rows):
                turned = turn_s[half, pl.ds(h, 2 * owners, stride=pitch), :].T
                for place in range(2):
                    kk = place if half == 0 else 1 - place
                    spec_s[kk, pl.ds(half * part * pitch + h, part, stride=pitch), :] = turned[
                        place * part : (place + 1) * part
                    ]
            for first in range(half * part, (half + 1) * part, chan_block):
                spec = []
                for c in range(first, first + chan_block):
                    start = c * pitch
                    both = [spec_s[kk, start : start + rows, :].astype(BF16) for kk in range(2)]
                    spec.append(jnp.concatenate(both, axis=1))
                mixed = jnp.dot(jnp.concatenate(spec, axis=0), table_ref[...], preferred_element_type=F32)
                block = pl.ds(first, chan_block)
                done_s[which, block] = mixed.astype(BF16).reshape(chan_block, rows, -1)
                copies.append(
                    pltpu.make_async_copy(done_s.at[which, block], out_ref.at[which, block], sems.at[len(copies)])
                )
                copies[-1].start()
    for copy in copies:
        copy.wait()


def inverse_rows(received, table):
    slices, owners, two_rows, wide = received.shape
    rows = two_rows // 2
    channels = wide // 2
    two_k, width = table.shape
    chan_block = min(16, channels)
    pitch = rows + 8
    vmem = pl.BlockSpec(memory_space=pltpu.VMEM)
    return pl.pallas_call(
        functools.partial(inverse_kernel, chan_block, pitch),
        in_specs=[vmem, vmem],
        out_specs=pl.BlockSpec(memory_space=pltpu.HBM),
        out_shape=jax.ShapeDtypeStruct((slices, channels, rows, width), BF16),
        scratch_shapes=[
            pltpu.VMEM((2, (two_k // 2 + 1) * pitch, channels), F32),
            pltpu.VMEM((2, (channels + 1) * pitch, two_k // 2), F32),
            pltpu.VMEM((slices, channels, rows, width), BF16),
            pltpu.SemaphoreType.DMA((slices * channels // chan_block,)),
        ],
        compiler_params=pltpu.CompilerParams(vmem_limit_bytes=40 * MIB),
        cost_estimate=pl.CostEstimate(
            flops=2 * slices * channels * rows * width * two_k,
            bytes_accessed=2 * slices * channels * rows * width,
            transcendentals=0,
        ),
        name="inverse_row_dft",
    )(received, table)


def exchange(blocks):
    shape = blocks.shape
    flat = blocks.reshape((shape[0] * shape[1],) + shape[2:])
    flat = lax.all_to_all(flat, ("blk", "row"), split_axis=0, concat_axis=0, tiled=True)
    return flat.reshape(shape)


def local(field, gain, w_first, b_first, w_second, b_second):
    slices, channels, rows, width = field.shape
    owners = lax.axis_size("row")
    modes_x = 2 * owners
    height = owners * rows
    fwd, inv = height_tables(height)
    spread = jnp.asarray(np.tile(np.eye(BLOCK_CH), (1, channels // BLOCK_CH)), BF16)
    table = jnp.asarray(forward_table(width, modes_x))

    swap = [(0, 1), (1, 0)]
    cut = width // 4
    groups = (((0, 0, width), (1, 0, cut)), ((1, cut, width - cut),))
    (held_first, own_first), (held_second, own_second) = [channel_stats(field, group) for group in groups]
    other_first = lax.ppermute(own_first, "blk", swap)
    other_second = lax.ppermute(own_second, "blk", swap)
    send, part = forward_rows(forward_first, held_first, gain, own_first, other_first, table, owners)
    send = forward_rows(
        forward_second, held_second, gain, own_second, other_second, table, owners, (part, send)
    )
    columns = exchange(send)
    filtered = filter_columns(
        columns, jnp.asarray(fwd), jnp.asarray(inv), spread, w_first, b_first, w_second, b_second
    )
    colfield = exchange(filtered)
    return inverse_rows(colfield, jnp.asarray(inverse_table(width, modes_x)))


def solution(mesh):
    return jax.shard_map(
        local,
        mesh=mesh,
        in_specs=(P(None, "blk", "row", None), P("blk"), P(), P(), P(), P()),
        out_specs=P(None, "blk", "row", None),
        check_vma=False,
    )
```

```python
import functools
import math

import jax
import jax.numpy as jnp
import ml_dtypes
import numpy as np
from jax import lax
from jax.experimental import pallas as pl
from jax.experimental.pallas import tpu as pltpu
from jax.sharding import PartitionSpec as P

BLOCK_CH = 32
EPS = 1e-05
SHRINK = 0.01
BF16 = jnp.bfloat16
F32 = jnp.float32
MIB = 1 << 20


def _angles(first, second, count):
    phase = np.mod(np.outer(first, second), count)
    return phase.astype(np.float32) * np.float32(2.0 * math.pi / count)


def _bf16(values):
    return np.asarray(values, np.float32).astype(ml_dtypes.bfloat16)


def mode_order(modes):
    return np.arange(modes).reshape(-1, 2).T.reshape(-1)


def forward_table(count, modes):
    t = _angles(np.arange(count), mode_order(modes), count)
    scale = np.float32(1.0 / math.sqrt(count))
    return _bf16(np.concatenate([np.cos(t) * scale, -np.sin(t) * scale], axis=1))


def inverse_table(count, modes):
    order = mode_order(modes)
    t = _angles(order, np.arange(count), count)
    weight = np.where(order == 0, 1.0, 2.0)[:, None].astype(np.float32)
    weight = weight * np.float32(1.0 / math.sqrt(count))
    both = np.stack([np.cos(t) * weight, -np.sin(t) * weight])
    both = both.reshape(2, 2, modes // 2, count).transpose(1, 0, 2, 3)
    return _bf16(both.reshape(2 * modes, count))


def height_tables(height):
    quarter = height // 4
    s = _angles(np.arange(quarter + 1), np.arange(height), height)
    scale = np.float32(1.0 / math.sqrt(height))
    cosine, sine = np.cos(s) * scale, np.sin(s) * scale
    last = np.zeros((16, height), np.float32)
    last[0], last[1] = cosine[quarter], sine[quarter]
    forward = np.concatenate([cosine[:quarter], sine[:quarter], last], axis=0)
    inverse = np.concatenate([cosine[:quarter].T, sine[:quarter].T], axis=1)
    return _bf16(forward), _bf16(inverse)


STEP = 16


def copies_of(segments, x_ref, held_refs, sems):
    found = []
    taken = 0
    for (which, first, lanes), ref in zip(segments, held_refs):
        channels, _, width = x_ref.shape[1], x_ref.shape[2], x_ref.shape[3]
        size = STEP * max(1, width // lanes)
        copies = []
        for c in range(0, channels, size):
            part = pl.ds(c, size)
            source = x_ref.at[which, part, :, pl.ds(first, lanes)]
            copies.append(pltpu.make_async_copy(source, ref.at[part], sems.at[taken]))
            taken += 1
        found.append((copies, size))
    return found


def stats_kernel(segments, x_ref, *refs):
    held_refs = refs[: len(segments)]
    stat_ref, pivot_s, first_s, second_s, sems = refs[len(segments) :]
    channels = x_ref.shape[1]
    rows = x_ref.shape[2]
    segment_copies = copies_of(segments, x_ref, held_refs, sems)
    for copies, _ in segment_copies:
        for copy in copies:
            copy.start()
    base = 0
    for (_, _, lanes), ref, (copies, size) in zip(segments, held_refs, segment_copies):
        wide = 512 if lanes % 512 == 0 else min(256, lanes)
        for at in range(0, channels, STEP):
            if at % size == 0:
                copies[at // size].wait()
            for lane in range(0, lanes, wide):
                there = slice(lane, lane + wide)
                here = slice(base + lane, base + lane + wide)
                if at == 0:
                    pivot = jnp.zeros((rows, wide), F32)
                    for c in range(STEP):
                        pivot = pivot + ref[c, :, there].astype(F32)
                    pivot = (pivot * (1.0 / STEP)).astype(BF16)
                    pivot_s[:, here] = pivot
                    first = jnp.zeros((rows, wide), F32)
                    second = jnp.zeros((rows, wide), F32)
                else:
                    pivot, first, second = pivot_s[:, here], first_s[:, here], second_s[:, here]
                for c in range(at, at + STEP, 2):
                    one = ref[c, :, there] - pivot
                    two = ref[c + 1, :, there] - pivot
                    one, two = one.astype(F32), two.astype(F32)
                    first = first + (one + two)
                    second = second + (one * one + two * two)
                if at + STEP < channels:
                    first_s[:, here], second_s[:, here] = first, second
                else:
                    offset = first * (1.0 / channels)
                    mean = pivot.astype(F32) + offset
                    high = mean.astype(BF16)
                    stat_ref[0, :, here] = high
                    stat_ref[1, :, here] = (mean - high.astype(F32)).astype(BF16)
                    stat_ref[2, :, here] = jnp.maximum(second - first * offset, 0.0).astype(BF16)
        base += lanes


def channel_stats(field, segments):
    _, channels, rows, width = field.shape
    total = sum(lanes for _, _, lanes in segments)
    count = sum(channels // (STEP * max(1, width // lanes)) for _, _, lanes in segments)
    vmem = pl.BlockSpec(memory_space=pltpu.VMEM)
    *held, stat = pl.pallas_call(
        functools.partial(stats_kernel, segments),
        in_specs=[pl.BlockSpec(memory_space=pltpu.HBM)],
        out_specs=[vmem] * (len(segments) + 1),
        out_shape=[jax.ShapeDtypeStruct((channels, rows, lanes), BF16) for _, _, lanes in segments]
        + [jax.ShapeDtypeStruct((3, rows, total), BF16)],
        scratch_shapes=[
            pltpu.VMEM((rows, total), BF16),
            pltpu.VMEM((rows, total), F32),
            pltpu.VMEM((rows, total), F32),
            pltpu.SemaphoreType.DMA((count,)),
        ],
        compiler_params=pltpu.CompilerParams(vmem_limit_bytes=16 * MIB),
        cost_estimate=pl.CostEstimate(
            flops=5 * channels * rows * total, bytes_accessed=2 * channels * rows * total, transcendentals=0
        ),
        name="channel_stats",
    )(pltpu.with_memory_space_constraint(field, pltpu.HBM))
    return held, stat


def normalizer(own_ref, other_ref, here, channels):
    own_mean = own_ref[0, :, here].astype(F32) + own_ref[1, :, here].astype(F32)
    other_mean = other_ref[0, :, here].astype(F32) + other_ref[1, :, here].astype(F32)
    delta = own_mean - other_mean
    moment = own_ref[2, :, here].astype(F32) + other_ref[2, :, here].astype(F32) + delta * delta * (channels * 0.5)
    return (own_mean + other_mean) * 0.5, lax.rsqrt(moment * (0.5 / channels) + EPS)


def project(x_ref, stats, table_ref, first_row, pitch, add_ref, spec_ref, chan_block=32):
    channels, rows, lanes = x_ref.shape
    parts, _, half = spec_ref.shape
    mean, scale = stats
    table = table_ref[first_row : first_row + lanes, :]
    for first in range(0, channels, chan_block):
        field = x_ref[first : first + chan_block].astype(F32)
        normed = ((field - mean[None]) * scale[None]).astype(BF16)
        spec = jnp.dot(normed.reshape(chan_block * rows, lanes), table, preferred_element_type=F32)
        for c in range(chan_block):
            start = (first + c) * pitch
            for p in range(parts):
                value = spec[c * rows : (c + 1) * rows, p * half : (p + 1) * half]
                if add_ref is not None:
                    value = value + add_ref[p, start : start + rows, :]
                spec_ref[p, start : start + rows, :] = value
        yield


def hand_out(which, gain_ref, spec_s, turn_s, send_ref, rows, pitch, beside=()):
    parts, _, half = spec_s.shape
    channels = turn_s.shape[-1]
    owners = send_ref.shape[1]
    beside = iter(beside)
    for h in range(rows):
        if h % 4 == 0:
            next(beside, None)
        for p in range(parts):
            turned = spec_s[p, pl.ds(h, channels, stride=pitch), :].T * gain_ref[...]
            turn_s[pl.ds(p * half * pitch + h, half, stride=pitch), :] = turned
    for _ in beside:
        pass
    for r in range(2):
        for kk in range(2):
            for d in range(owners):
                start = ((r * 2 + kk) * owners + d) * pitch
                send_ref[which, d, r * rows : (r + 1) * rows, kk * channels : (kk + 1) * channels] = turn_s[
                    start : start + rows, :
                ].astype(BF16)


def forward_first(pitch, x_ref, early_ref, gain_ref, own_ref, other_ref, table_ref, send_ref, part_ref, spec_s, turn_s):
    channels, rows, width = x_ref.shape
    cut = early_ref.shape[2]
    stats = normalizer(own_ref, other_ref, slice(0, width), channels)
    for _ in project(x_ref, stats, table_ref, 0, pitch, None, spec_s):
        pass
    stats = normalizer(own_ref, other_ref, slice(width, width + cut), channels)
    early = project(early_ref, stats, table_ref, 0, pitch, None, part_ref)
    hand_out(0, gain_ref, spec_s, turn_s, send_ref, rows, pitch, early)


def forward_second(pitch, x_ref, gain_ref, own_ref, other_ref, table_ref, part_ref, _, send_ref, spec_s, turn_s):
    channels, rows, lanes = x_ref.shape
    cut = table_ref.shape[0] - lanes
    stats = normalizer(own_ref, other_ref, slice(0, lanes), channels)
    for _ in project(x_ref, stats, table_ref, cut, pitch, part_ref, spec_s):
        pass
    hand_out(1, gain_ref, spec_s, turn_s, send_ref, rows, pitch)


def forward_rows(kernel, held, gain, own, other, table, owners, more=()):
    channels, rows, _ = held[0].shape
    width, two_k = table.shape
    pitch = rows + 8
    vmem = pl.BlockSpec(memory_space=pltpu.VMEM)
    send = jax.ShapeDtypeStruct((2, owners, 2 * rows, 2 * channels), BF16)
    part = jax.ShapeDtypeStruct((2, (channels + 1) * pitch, two_k // 2), F32)
    lanes = sum(x.shape[2] for x in held)
    return pl.pallas_call(
        functools.partial(kernel, pitch),
        in_specs=[vmem] * (len(held) + 4 + len(more)),
        out_specs=vmem if more else [vmem, vmem],
        out_shape=send if more else [send, part],
        scratch_shapes=[
            pltpu.VMEM((2, (channels + 1) * pitch, two_k // 2), F32),
            pltpu.VMEM(((two_k + 1) * pitch, channels), F32),
        ],
        input_output_aliases={len(held) + 5: 0} if more else {},
        compiler_params=pltpu.CompilerParams(vmem_limit_bytes=24 * MIB),
        cost_estimate=pl.CostEstimate(
            flops=2 * channels * rows * lanes * two_k, bytes_accessed=2 * channels * rows * lanes, transcendentals=0
        ),
        name="norm_and_row_dft",
    )(*held, gain.reshape(1, channels), own, other, table, *more)


def block_diagonal(weights, spread, lanes):
    tiled = jnp.dot(weights, spread, preferred_element_type=F32)
    row = lax.broadcasted_iota(jnp.int32, (lanes, lanes), 0) // BLOCK_CH
    col = lax.broadcasted_iota(jnp.int32, (lanes, lanes), 1) // BLOCK_CH
    return jnp.where(row == col, tiled, 0.0)


def fill_weights(w_ref, group, spread, big, lanes, turned=None):
    mine = slice(group * lanes, (group + 1) * lanes)
    real = block_diagonal(w_ref[0, mine, :], spread, lanes)
    imag = block_diagonal(w_ref[1, mine, :], spread, lanes)
    for target, shift in ((big, 0), (turned, lanes // 2)):
        if target is not None:
            re = pltpu.roll(real, shift, 1) if shift else real
            im = pltpu.roll(imag, shift, 1) if shift else imag
            target[:lanes, :lanes] = re.astype(BF16)
            target[:lanes, lanes:] = im.astype(BF16)
            target[lanes:, :lanes] = (-im).astype(BF16)
            target[lanes:, lanes:] = re.astype(BF16)


def bias_row(b_ref, group, lanes, shift=0):
    mine = slice(group * lanes, (group + 1) * lanes)
    both = [b_ref[0:1, mine], b_ref[1:2, mine]]
    if shift:
        both = [pltpu.roll(b, shift, 1) for b in both]
    return jnp.concatenate(both, axis=1)


def filter_kernel(x_ref, fwd_ref, inv_ref, spread_ref, w1_ref, b1_ref, w2_ref, b2_ref, out_ref, big1, big2, big2_turned, spec_s, packed):
    groups, owners, two_rows, wide = x_ref.shape
    rows = two_rows // 2
    lanes = wide // 2
    height = owners * rows
    quarter = height // 4
    top = lax.broadcasted_iota(jnp.int32, (quarter, lanes), 0) == 0
    turn = lax.broadcasted_iota(jnp.int32, (8, 1), 0) % 4
    norm = 1.0 / math.sqrt(height)
    last_cos = jnp.where(turn == 0, norm, jnp.where(turn == 2, -norm, 0.0))
    last_sin = jnp.where(turn == 1, norm, jnp.where(turn == 3, -norm, 0.0))
    real_part = lambda kk: slice(kk * lanes, (kk + 1) * lanes)

    def transform(group):
        real_in = x_ref[group, :, :rows, :].reshape(height, wide)
        imag_in = x_ref[group, :, rows:, :].reshape(height, wide)
        from_real = jnp.dot(fwd_ref[...], real_in, preferred_element_type=F32)
        from_imag = jnp.dot(fwd_ref[...], imag_in, preferred_element_type=F32)
        last = slice(2 * quarter, 2 * quarter + 1)
        last_sine = slice(2 * quarter + 1, 2 * quarter + 2)
        for kk in range(2):
            part = real_part(kk)
            cos_re, sin_re = from_real[:quarter, part], from_real[quarter : 2 * quarter, part]
            cos_im, sin_im = from_imag[:quarter, part], from_imag[quarter : 2 * quarter, part]
            last_re = from_real[last, part] - from_imag[last_sine, part]
            last_im = from_imag[last, part] + from_real[last_sine, part]
            spec_s[group, kk, :quarter, :lanes] = (cos_re + sin_im).astype(BF16)
            spec_s[group, kk, :quarter, lanes:] = (cos_im - sin_re).astype(BF16)
            spec_s[group, kk, quarter:, :lanes] = jnp.where(top, last_re, cos_re - sin_im).astype(BF16)
            spec_s[group, kk, quarter:, lanes:] = jnp.where(top, last_im, cos_im + sin_re).astype(BF16)

    def mix(group):
        values, extras = [], []
        for kk in range(2):
            shift = kk * (lanes // 2)
            second = (big2 if kk == 0 else big2_turned)[group]
            hidden = jnp.dot(spec_s[group, kk], big1[group], preferred_element_type=F32) + bias_row(b1_ref, group, lanes)
            hidden = jnp.maximum(hidden, 0.0).astype(BF16)
            mixed = jnp.dot(hidden, second, preferred_element_type=F32) + bias_row(b2_ref, group, lanes, shift)
            kept = mixed - jnp.clip(mixed, -SHRINK, SHRINK)
            plus_re, plus_im = kept[:quarter, :lanes], kept[:quarter, lanes:]
            minus_re, minus_im = kept[quarter:, :lanes], kept[quarter:, lanes:]
            last_re, last_im = minus_re[0:1], minus_im[0:1]
            minus_re = jnp.where(top, 0.0, minus_re)
            minus_im = jnp.where(top, 0.0, minus_im)
            values.append([plus_re + minus_re, plus_im + minus_im, minus_im - plus_im, plus_re - minus_re])
            extras.append([last_cos * last_re + last_sin * last_im, last_cos * last_im - last_sin * last_re])

        def halves(zero, one):
            low = lax.broadcasted_iota(jnp.int32, zero.shape, 1) < lanes // 2
            return jnp.where(low, zero, one), jnp.where(low, one, zero)

        for i, (zero, one) in enumerate(zip(*values)):
            for half, value in enumerate(halves(zero, one)):
                start = (i % 2) * wide + half * lanes
                packed[group, (i // 2) * quarter : (i // 2 + 1) * quarter, start : start + lanes] = value.astype(BF16)
        return jnp.concatenate([part for zero, one in zip(*extras) for part in halves(zero, one)], axis=1)

    def invert(group, extra):
        column = jnp.dot(inv_ref[...], packed[group], preferred_element_type=F32)
        column = (column.reshape(height // 8, 8, 2 * wide) + extra[None]).astype(BF16)
        column = column.reshape(height, 2 * wide)
        out_ref[group, :, :rows, :] = column[:, :wide].reshape(owners, rows, wide)
        out_ref[group, :, rows:, :] = column[:, wide:].reshape(owners, rows, wide)

    for group in range(groups):
        fill_weights(w1_ref, group, spread_ref[...], big1.at[group], lanes)
        fill_weights(w2_ref, group, spread_ref[...], big2.at[group], lanes, big2_turned.at[group])
    for group in range(groups):
        transform(group)
    extra = [mix(group) for group in range(groups)]
    for group in range(groups):
        invert(group, extra[group])


def filter_columns(received, fwd, inv, spread, w_first, b_first, w_second, b_second):
    groups, owners, two_rows, wide = received.shape
    height = owners * two_rows // 2
    vmem = pl.BlockSpec(memory_space=pltpu.VMEM)

    def flat(w):
        return w.reshape(2, -1, BLOCK_CH)

    return pl.pallas_call(
        filter_kernel,
        in_specs=[vmem] * 8,
        out_specs=vmem,
        out_shape=jax.ShapeDtypeStruct(received.shape, BF16),
        scratch_shapes=[
            pltpu.VMEM((groups, wide, wide), BF16),
            pltpu.VMEM((groups, wide, wide), BF16),
            pltpu.VMEM((groups, wide, wide), BF16),
            pltpu.VMEM((groups, 2, height // 2, wide), BF16),
            pltpu.VMEM((groups, height // 2, 2 * wide), BF16),
        ],
        compiler_params=pltpu.CompilerParams(vmem_limit_bytes=40 * MIB),
        cost_estimate=pl.CostEstimate(
            flops=2 * groups * height * wide * 3 * height, bytes_accessed=8 * MIB, transcendentals=0
        ),
        name="column_filter",
    )(received, fwd, inv, spread, flat(w_first), b_first, flat(w_second), b_second)


def inverse_kernel(chan_block, pitch, x_ref, table_ref, out_ref, turn_s, spec_s, done_s, sems):
    slices, owners, two_rows, wide = x_ref.shape
    rows = two_rows // 2
    lanes = wide // 2
    part = lanes // 2
    copies = []
    for which in range(slices):
        for half in range(2):
            for r in range(2):
                for d in range(owners):
                    start = (r * owners + d) * pitch
                    turn_s[half, start : start + rows, :] = x_ref[
                        which, d, r * rows : (r + 1) * rows, half * lanes : (half + 1) * lanes
                    ].astype(F32)
            for h in range(rows):
                turned = turn_s[half, pl.ds(h, 2 * owners, stride=pitch), :].T
                for place in range(2):
                    kk = place if half == 0 else 1 - place
                    spec_s[kk, pl.ds(half * part * pitch + h, part, stride=pitch), :] = turned[
                        place * part : (place + 1) * part
                    ]
            for first in range(half * part, (half + 1) * part, chan_block):
                spec = []
                for c in range(first, first + chan_block):
                    start = c * pitch
                    both = [spec_s[kk, start : start + rows, :].astype(BF16) for kk in range(2)]
                    spec.append(jnp.concatenate(both, axis=1))
                mixed = jnp.dot(jnp.concatenate(spec, axis=0), table_ref[...], preferred_element_type=F32)
                block = pl.ds(first, chan_block)
                done_s[which, block] = mixed.astype(BF16).reshape(chan_block, rows, -1)
                copies.append(
                    pltpu.make_async_copy(done_s.at[which, block], out_ref.at[which, block], sems.at[len(copies)])
                )
                copies[-1].start()
    for copy in copies:
        copy.wait()


def inverse_rows(received, table):
    slices, owners, two_rows, wide = received.shape
    rows = two_rows // 2
    channels = wide // 2
    two_k, width = table.shape
    chan_block = min(16, channels)
    pitch = rows + 8
    vmem = pl.BlockSpec(memory_space=pltpu.VMEM)
    return pl.pallas_call(
        functools.partial(inverse_kernel, chan_block, pitch),
        in_specs=[vmem, vmem],
        out_specs=pl.BlockSpec(memory_space=pltpu.HBM),
        out_shape=jax.ShapeDtypeStruct((slices, channels, rows, width), BF16),
        scratch_shapes=[
            pltpu.VMEM((2, (two_k // 2 + 1) * pitch, channels), F32),
            pltpu.VMEM((2, (channels + 1) * pitch, two_k // 2), F32),
            pltpu.VMEM((slices, channels, rows, width), BF16),
            pltpu.SemaphoreType.DMA((slices * channels // chan_block,)),
        ],
        compiler_params=pltpu.CompilerParams(vmem_limit_bytes=40 * MIB),
        cost_estimate=pl.CostEstimate(
            flops=2 * slices * channels * rows * width * two_k,
            bytes_accessed=2 * slices * channels * rows * width,
            transcendentals=0,
        ),
        name="inverse_row_dft",
    )(received, table)


def exchange(blocks):
    shape = blocks.shape
    flat = blocks.reshape((shape[0] * shape[1],) + shape[2:])
    flat = lax.all_to_all(flat, ("blk", "row"), split_axis=0, concat_axis=0, tiled=True)
    return flat.reshape(shape)


def local(field, gain, w_first, b_first, w_second, b_second):
    slices, channels, rows, width = field.shape
    owners = lax.axis_size("row")
    modes_x = 2 * owners
    height = owners * rows
    fwd, inv = height_tables(height)
    spread = jnp.asarray(np.tile(np.eye(BLOCK_CH), (1, channels // BLOCK_CH)), BF16)
    table = jnp.asarray(forward_table(width, modes_x))

    swap = [(0, 1), (1, 0)]
    cut = width // 4
    groups = (((0, 0, width), (1, 0, cut)), ((1, cut, width - cut),))
    (held_first, own_first), (held_second, own_second) = [channel_stats(field, group) for group in groups]
    other_first = lax.ppermute(own_first, "blk", swap)
    other_second = lax.ppermute(own_second, "blk", swap)
    send, part = forward_rows(forward_first, held_first, gain, own_first, other_first, table, owners)
    send = forward_rows(
        forward_second, held_second, gain, own_second, other_second, table, owners, (part, send)
    )
    columns = exchange(send)
    filtered = filter_columns(
        columns, jnp.asarray(fwd), jnp.asarray(inv), spread, w_first, b_first, w_second, b_second
    )
    colfield = exchange(filtered)
    return inverse_rows(colfield, jnp.asarray(inverse_table(width, modes_x)))


def solution(mesh):
    return jax.shard_map(
        local,
        mesh=mesh,
        in_specs=(P(None, "blk", "row", None), P("blk"), P(), P(), P(), P()),
        out_specs=P(None, "blk", "row", None),
        check_vma=False,
    )
```

```python
import functools
import math

import jax
import jax.numpy as jnp
import ml_dtypes
import numpy as np
from jax import lax
from jax.experimental import pallas as pl
from jax.experimental.pallas import tpu as pltpu
from jax.sharding import PartitionSpec as P

BLOCK_CH = 32
EPS = 1e-05
SHRINK = 0.01
BF16 = jnp.bfloat16
F32 = jnp.float32
MIB = 1 << 20


def _angles(first, second, count):
    phase = np.mod(np.outer(first, second), count)
    return phase.astype(np.float32) * np.float32(2.0 * math.pi / count)


def _bf16(values):
    return np.asarray(values, np.float32).astype(ml_dtypes.bfloat16)


def mode_order(modes):
    return np.arange(modes).reshape(-1, 2).T.reshape(-1)


def forward_table(count, modes):
    t = _angles(np.arange(count), mode_order(modes), count)
    scale = np.float32(1.0 / math.sqrt(count))
    return _bf16(np.concatenate([np.cos(t) * scale, -np.sin(t) * scale], axis=1))


def inverse_table(count, modes):
    order = mode_order(modes)
    t = _angles(order, np.arange(count), count)
    weight = np.where(order == 0, 1.0, 2.0)[:, None].astype(np.float32)
    weight = weight * np.float32(1.0 / math.sqrt(count))
    both = np.stack([np.cos(t) * weight, -np.sin(t) * weight])
    both = both.reshape(2, 2, modes // 2, count).transpose(1, 0, 2, 3)
    return _bf16(both.reshape(2 * modes, count))


def height_tables(height):
    quarter = height // 4
    s = _angles(np.arange(quarter + 1), np.arange(height), height)
    scale = np.float32(1.0 / math.sqrt(height))
    cosine, sine = np.cos(s) * scale, np.sin(s) * scale
    last = np.zeros((16, height), np.float32)
    last[0], last[1] = cosine[quarter], sine[quarter]
    forward = np.concatenate([cosine[:quarter], sine[:quarter], last], axis=0)
    inverse = np.concatenate([cosine[:quarter].T, sine[:quarter].T], axis=1)
    return _bf16(forward), _bf16(inverse)


STEP = 16


def copies_of(segments, x_ref, held_refs, sems):
    found = []
    taken = 0
    for (which, first, lanes), ref in zip(segments, held_refs):
        channels, _, width = x_ref.shape[1], x_ref.shape[2], x_ref.shape[3]
        size = STEP * max(1, width // lanes)
        copies = []
        for c in range(0, channels, size):
            part = pl.ds(c, size)
            source = x_ref.at[which, part, :, pl.ds(first, lanes)]
            copies.append(pltpu.make_async_copy(source, ref.at[part], sems.at[taken]))
            taken += 1
        found.append((copies, size))
    return found


def stats_kernel(segments, x_ref, *refs):
    held_refs = refs[: len(segments)]
    stat_ref, pivot_s, first_s, second_s, sems = refs[len(segments) :]
    channels = x_ref.shape[1]
    rows = x_ref.shape[2]
    segment_copies = copies_of(segments, x_ref, held_refs, sems)
    for copies, _ in segment_copies:
        for copy in copies:
            copy.start()
    base = 0
    for (_, _, lanes), ref, (copies, size) in zip(segments, held_refs, segment_copies):
        wide = 512 if lanes % 512 == 0 else min(256, lanes)
        for at in range(0, channels, STEP):
            if at % size == 0:
                copies[at // size].wait()
            for lane in range(0, lanes, wide):
                there = slice(lane, lane + wide)
                here = slice(base + lane, base + lane + wide)
                if at == 0:
                    pivot = jnp.zeros((rows, wide), F32)
                    for c in range(STEP):
                        pivot = pivot + ref[c, :, there].astype(F32)
                    pivot = (pivot * (1.0 / STEP)).astype(BF16)
                    pivot_s[:, here] = pivot
                    first = jnp.zeros((rows, wide), F32)
                    second = jnp.zeros((rows, wide), F32)
                else:
                    pivot, first, second = pivot_s[:, here], first_s[:, here], second_s[:, here]
                for c in range(at, at + STEP, 2):
                    one = ref[c, :, there] - pivot
                    two = ref[c + 1, :, there] - pivot
                    one, two = one.astype(F32), two.astype(F32)
                    first = first + (one + two)
                    second = second + (one * one + two * two)
                if at + STEP < channels:
                    first_s[:, here], second_s[:, here] = first, second
                else:
                    offset = first * (1.0 / channels)
                    mean = pivot.astype(F32) + offset
                    high = mean.astype(BF16)
                    stat_ref[0, :, here] = high
                    stat_ref[1, :, here] = (mean - high.astype(F32)).astype(BF16)
                    stat_ref[2, :, here] = jnp.maximum(second - first * offset, 0.0).astype(BF16)
        base += lanes


def channel_stats(field, segments):
    _, channels, rows, width = field.shape
    total = sum(lanes for _, _, lanes in segments)
    count = sum(channels // (STEP * max(1, width // lanes)) for _, _, lanes in segments)
    vmem = pl.BlockSpec(memory_space=pltpu.VMEM)
    *held, stat = pl.pallas_call(
        functools.partial(stats_kernel, segments),
        in_specs=[pl.BlockSpec(memory_space=pltpu.HBM)],
        out_specs=[vmem] * (len(segments) + 1),
        out_shape=[jax.ShapeDtypeStruct((channels, rows, lanes), BF16) for _, _, lanes in segments]
        + [jax.ShapeDtypeStruct((3, rows, total), BF16)],
        scratch_shapes=[
            pltpu.VMEM((rows, total), BF16),
            pltpu.VMEM((rows, total), F32),
            pltpu.VMEM((rows, total), F32),
            pltpu.SemaphoreType.DMA((count,)),
        ],
        compiler_params=pltpu.CompilerParams(vmem_limit_bytes=16 * MIB),
        cost_estimate=pl.CostEstimate(
            flops=5 * channels * rows * total, bytes_accessed=2 * channels * rows * total, transcendentals=0
        ),
        name="channel_stats",
    )(pltpu.with_memory_space_constraint(field, pltpu.HBM))
    return held, stat


def normalizer(own_ref, other_ref, here, channels):
    own_mean = own_ref[0, :, here].astype(F32) + own_ref[1, :, here].astype(F32)
    other_mean = other_ref[0, :, here].astype(F32) + other_ref[1, :, here].astype(F32)
    delta = own_mean - other_mean
    moment = own_ref[2, :, here].astype(F32) + other_ref[2, :, here].astype(F32) + delta * delta * (channels * 0.5)
    return (own_mean + other_mean) * 0.5, lax.rsqrt(moment * (0.5 / channels) + EPS)


def project(x_ref, stats, table_ref, first_row, pitch, add_ref, spec_ref, chan_block=32):
    channels, rows, lanes = x_ref.shape
    parts, _, half = spec_ref.shape
    mean, scale = stats
    table = table_ref[first_row : first_row + lanes, :]
    for first in range(0, channels, chan_block):
        field = x_ref[first : first + chan_block].astype(F32)
        normed = ((field - mean[None]) * scale[None]).astype(BF16)
        spec = jnp.dot(normed.reshape(chan_block * rows, lanes), table, preferred_element_type=F32)
        for c in range(chan_block):
            start = (first + c) * pitch
            for p in range(parts):
                value = spec[c * rows : (c + 1) * rows, p * half : (p + 1) * half]
                if add_ref is not None:
                    value = value + add_ref[p, start : start + rows, :]
                spec_ref[p, start : start + rows, :] = value
        yield


def hand_out(gain_ref, spec_s, turn_s, slice_ref, rows, pitch, beside=()):
    parts, _, half = spec_s.shape
    channels = turn_s.shape[-1]
    owners = slice_ref.shape[0]
    beside = iter(beside)
    for h in range(rows):
        if h % 4 == 0:
            next(beside, None)
        for p in range(parts):
            turned = spec_s[p, pl.ds(h, channels, stride=pitch), :].T * gain_ref[...]
            turn_s[pl.ds(p * half * pitch + h, half, stride=pitch), :] = turned
    for _ in beside:
        pass
    for r in range(2):
        for kk in range(2):
            for d in range(owners):
                start = ((r * 2 + kk) * owners + d) * pitch
                slice_ref[d, r * rows : (r + 1) * rows, kk * channels : (kk + 1) * channels] = turn_s[
                    start : start + rows, :
                ].astype(BF16)


def forward_first(pitch, x_ref, early_ref, gain_ref, own_ref, other_ref, table_ref, first_ref, part_ref, spec_s, turn_s):
    channels, rows, width = x_ref.shape
    cut = early_ref.shape[2]
    stats = normalizer(own_ref, other_ref, slice(0, width), channels)
    for _ in project(x_ref, stats, table_ref, 0, pitch, None, spec_s):
        pass
    stats = normalizer(own_ref, other_ref, slice(width, width + cut), channels)
    early = project(early_ref, stats, table_ref, 0, pitch, None, part_ref)
    hand_out(gain_ref, spec_s, turn_s, first_ref, rows, pitch, early)


def forward_second(
    pitch, x_ref, gain_ref, own_ref, other_ref, table_ref, first_ref, part_ref, send_ref, spec_s, turn_s, sem
):
    copy = pltpu.make_async_copy(first_ref, send_ref.at[0], sem)
    copy.start()
    channels, rows, lanes = x_ref.shape
    cut = table_ref.shape[0] - lanes
    stats = normalizer(own_ref, other_ref, slice(0, lanes), channels)
    for _ in project(x_ref, stats, table_ref, cut, pitch, part_ref, spec_s):
        pass
    hand_out(gain_ref, spec_s, turn_s, send_ref.at[1], rows, pitch)
    copy.wait()


def forward_rows(kernel, held, gain, own, other, table, owners, more=()):
    channels, rows, _ = held[0].shape
    width, two_k = table.shape
    pitch = rows + 8
    vmem = pl.BlockSpec(memory_space=pltpu.VMEM)
    one = (owners, 2 * rows, 2 * channels)
    part = jax.ShapeDtypeStruct((2, (channels + 1) * pitch, two_k // 2), F32)
    lanes = sum(x.shape[2] for x in held)
    return pl.pallas_call(
        functools.partial(kernel, pitch),
        in_specs=[vmem] * (len(held) + 4 + len(more)),
        out_specs=vmem if more else [vmem, vmem],
        out_shape=jax.ShapeDtypeStruct((2,) + one, BF16) if more else [jax.ShapeDtypeStruct(one, BF16), part],
        scratch_shapes=[
            pltpu.VMEM((2, (channels + 1) * pitch, two_k // 2), F32),
            pltpu.VMEM(((two_k + 1) * pitch, channels), F32),
        ]
        + [pltpu.SemaphoreType.DMA] * (1 if more else 0),
        compiler_params=pltpu.CompilerParams(vmem_limit_bytes=24 * MIB),
        cost_estimate=pl.CostEstimate(
            flops=2 * channels * rows * lanes * two_k, bytes_accessed=2 * channels * rows * lanes, transcendentals=0
        ),
        name="norm_and_row_dft",
    )(*held, gain.reshape(1, channels), own, other, table, *more)


def block_diagonal(weights, spread, lanes):
    tiled = jnp.dot(weights, spread, preferred_element_type=F32)
    row = lax.broadcasted_iota(jnp.int32, (lanes, lanes), 0) // BLOCK_CH
    col = lax.broadcasted_iota(jnp.int32, (lanes, lanes), 1) // BLOCK_CH
    return jnp.where(row == col, tiled, 0.0)


def fill_weights(w_ref, group, spread, big, lanes, turned=None):
    mine = slice(group * lanes, (group + 1) * lanes)
    real = block_diagonal(w_ref[0, mine, :], spread, lanes)
    imag = block_diagonal(w_ref[1, mine, :], spread, lanes)
    for target, shift in ((big, 0), (turned, lanes // 2)):
        if target is not None:
            re = pltpu.roll(real, shift, 1) if shift else real
            im = pltpu.roll(imag, shift, 1) if shift else imag
            target[:lanes, :lanes] = re.astype(BF16)
            target[:lanes, lanes:] = im.astype(BF16)
            target[lanes:, :lanes] = (-im).astype(BF16)
            target[lanes:, lanes:] = re.astype(BF16)


def bias_row(b_ref, group, lanes, shift=0):
    mine = slice(group * lanes, (group + 1) * lanes)
    both = [b_ref[0:1, mine], b_ref[1:2, mine]]
    if shift:
        both = [pltpu.roll(b, shift, 1) for b in both]
    return jnp.concatenate(both, axis=1)


def filter_kernel(x_ref, fwd_ref, inv_ref, spread_ref, w1_ref, b1_ref, w2_ref, b2_ref, out_ref, big1, big2, big2_turned, spec_s, packed):
    groups, owners, two_rows, wide = x_ref.shape
    rows = two_rows // 2
    lanes = wide // 2
    height = owners * rows
    quarter = height // 4
    top = lax.broadcasted_iota(jnp.int32, (quarter, lanes), 0) == 0
    turn = lax.broadcasted_iota(jnp.int32, (8, 1), 0) % 4
    norm = 1.0 / math.sqrt(height)
    last_cos = jnp.where(turn == 0, norm, jnp.where(turn == 2, -norm, 0.0))
    last_sin = jnp.where(turn == 1, norm, jnp.where(turn == 3, -norm, 0.0))
    real_part = lambda kk: slice(kk * lanes, (kk + 1) * lanes)

    def transform(group):
        real_in = x_ref[group, :, :rows, :].reshape(height, wide)
        imag_in = x_ref[group, :, rows:, :].reshape(height, wide)
        from_real = jnp.dot(fwd_ref[...], real_in, preferred_element_type=F32)
        from_imag = jnp.dot(fwd_ref[...], imag_in, preferred_element_type=F32)
        last = slice(2 * quarter, 2 * quarter + 1)
        last_sine = slice(2 * quarter + 1, 2 * quarter + 2)
        for kk in range(2):
            part = real_part(kk)
            cos_re, sin_re = from_real[:quarter, part], from_real[quarter : 2 * quarter, part]
            cos_im, sin_im = from_imag[:quarter, part], from_imag[quarter : 2 * quarter, part]
            last_re = from_real[last, part] - from_imag[last_sine, part]
            last_im = from_imag[last, part] + from_real[last_sine, part]
            spec_s[group, kk, :quarter, :lanes] = (cos_re + sin_im).astype(BF16)
            spec_s[group, kk, :quarter, lanes:] = (cos_im - sin_re).astype(BF16)
            spec_s[group, kk, quarter:, :lanes] = jnp.where(top, last_re, cos_re - sin_im).astype(BF16)
            spec_s[group, kk, quarter:, lanes:] = jnp.where(top, last_im, cos_im + sin_re).astype(BF16)

    def mix(group):
        values, extras = [], []
        for kk in range(2):
            shift = kk * (lanes // 2)
            second = (big2 if kk == 0 else big2_turned)[group]
            hidden = jnp.dot(spec_s[group, kk], big1[group], preferred_element_type=F32) + bias_row(b1_ref, group, lanes)
            hidden = jnp.maximum(hidden, 0.0).astype(BF16)
            mixed = jnp.dot(hidden, second, preferred_element_type=F32) + bias_row(b2_ref, group, lanes, shift)
            kept = mixed - jnp.clip(mixed, -SHRINK, SHRINK)
            plus_re, plus_im = kept[:quarter, :lanes], kept[:quarter, lanes:]
            minus_re, minus_im = kept[quarter:, :lanes], kept[quarter:, lanes:]
            last_re, last_im = minus_re[0:1], minus_im[0:1]
            minus_re = jnp.where(top, 0.0, minus_re)
            minus_im = jnp.where(top, 0.0, minus_im)
            values.append([plus_re + minus_re, plus_im + minus_im, minus_im - plus_im, plus_re - minus_re])
            extras.append([last_cos * last_re + last_sin * last_im, last_cos * last_im - last_sin * last_re])

        def halves(zero, one):
            low = lax.broadcasted_iota(jnp.int32, zero.shape, 1) < lanes // 2
            return jnp.where(low, zero, one), jnp.where(low, one, zero)

        for i, (zero, one) in enumerate(zip(*values)):
            for half, value in enumerate(halves(zero, one)):
                start = (i % 2) * wide + half * lanes
                packed[group, (i // 2) * quarter : (i // 2 + 1) * quarter, start : start + lanes] = value.astype(BF16)
        return jnp.concatenate([part for zero, one in zip(*extras) for part in halves(zero, one)], axis=1)

    def invert(group, extra):
        column = jnp.dot(inv_ref[...], packed[group], preferred_element_type=F32)
        column = (column.reshape(height // 8, 8, 2 * wide) + extra[None]).astype(BF16)
        column = column.reshape(height, 2 * wide)
        out_ref[group, :, :rows, :] = column[:, :wide].reshape(owners, rows, wide)
        out_ref[group, :, rows:, :] = column[:, wide:].reshape(owners, rows, wide)

    for group in range(groups):
        fill_weights(w1_ref, group, spread_ref[...], big1.at[group], lanes)
        fill_weights(w2_ref, group, spread_ref[...], big2.at[group], lanes, big2_turned.at[group])
    for group in range(groups):
        transform(group)
    extra = [mix(group) for group in range(groups)]
    for group in range(groups):
        invert(group, extra[group])


def filter_columns(received, fwd, inv, spread, w_first, b_first, w_second, b_second):
    groups, owners, two_rows, wide = received.shape
    height = owners * two_rows // 2
    vmem = pl.BlockSpec(memory_space=pltpu.VMEM)

    def flat(w):
        return w.reshape(2, -1, BLOCK_CH)

    return pl.pallas_call(
        filter_kernel,
        in_specs=[vmem] * 8,
        out_specs=vmem,
        out_shape=jax.ShapeDtypeStruct(received.shape, BF16),
        scratch_shapes=[
            pltpu.VMEM((groups, wide, wide), BF16),
            pltpu.VMEM((groups, wide, wide), BF16),
            pltpu.VMEM((groups, wide, wide), BF16),
            pltpu.VMEM((groups, 2, height // 2, wide), BF16),
            pltpu.VMEM((groups, height // 2, 2 * wide), BF16),
        ],
        compiler_params=pltpu.CompilerParams(vmem_limit_bytes=40 * MIB),
        cost_estimate=pl.CostEstimate(
            flops=2 * groups * height * wide * 3 * height, bytes_accessed=8 * MIB, transcendentals=0
        ),
        name="column_filter",
    )(received, fwd, inv, spread, flat(w_first), b_first, flat(w_second), b_second)


def inverse_kernel(chan_block, pitch, x_ref, table_ref, out_ref, turn_s, spec_s, done_s, sems):
    slices, owners, two_rows, wide = x_ref.shape
    rows = two_rows // 2
    lanes = wide // 2
    part = lanes // 2
    copies = []
    for which in range(slices):
        for half in range(2):
            for r in range(2):
                for d in range(owners):
                    start = (r * owners + d) * pitch
                    turn_s[half, start : start + rows, :] = x_ref[
                        which, d, r * rows : (r + 1) * rows, half * lanes : (half + 1) * lanes
                    ].astype(F32)
            for h in range(rows):
                turned = turn_s[half, pl.ds(h, 2 * owners, stride=pitch), :].T
                for place in range(2):
                    kk = place if half == 0 else 1 - place
                    spec_s[kk, pl.ds(half * part * pitch + h, part, stride=pitch), :] = turned[
                        place * part : (place + 1) * part
                    ]
            for first in range(half * part, (half + 1) * part, chan_block):
                spec = []
                for c in range(first, first + chan_block):
                    start = c * pitch
                    both = [spec_s[kk, start : start + rows, :].astype(BF16) for kk in range(2)]
                    spec.append(jnp.concatenate(both, axis=1))
                mixed = jnp.dot(jnp.concatenate(spec, axis=0), table_ref[...], preferred_element_type=F32)
                block = pl.ds(first, chan_block)
                done_s[which, block] = mixed.astype(BF16).reshape(chan_block, rows, -1)
                copies.append(
                    pltpu.make_async_copy(done_s.at[which, block], out_ref.at[which, block], sems.at[len(copies)])
                )
                copies[-1].start()
    for copy in copies:
        copy.wait()


def inverse_rows(received, table):
    slices, owners, two_rows, wide = received.shape
    rows = two_rows // 2
    channels = wide // 2
    two_k, width = table.shape
    chan_block = min(16, channels)
    pitch = rows + 8
    vmem = pl.BlockSpec(memory_space=pltpu.VMEM)
    return pl.pallas_call(
        functools.partial(inverse_kernel, chan_block, pitch),
        in_specs=[vmem, vmem],
        out_specs=pl.BlockSpec(memory_space=pltpu.HBM),
        out_shape=jax.ShapeDtypeStruct((slices, channels, rows, width), BF16),
        scratch_shapes=[
            pltpu.VMEM((2, (two_k // 2 + 1) * pitch, channels), F32),
            pltpu.VMEM((2, (channels + 1) * pitch, two_k // 2), F32),
            pltpu.VMEM((slices, channels, rows, width), BF16),
            pltpu.SemaphoreType.DMA((slices * channels // chan_block,)),
        ],
        compiler_params=pltpu.CompilerParams(vmem_limit_bytes=40 * MIB),
        cost_estimate=pl.CostEstimate(
            flops=2 * slices * channels * rows * width * two_k,
            bytes_accessed=2 * slices * channels * rows * width,
            transcendentals=0,
        ),
        name="inverse_row_dft",
    )(received, table)


def exchange(blocks):
    shape = blocks.shape
    flat = blocks.reshape((shape[0] * shape[1],) + shape[2:])
    flat = lax.all_to_all(flat, ("blk", "row"), split_axis=0, concat_axis=0, tiled=True)
    return flat.reshape(shape)


def local(field, gain, w_first, b_first, w_second, b_second):
    slices, channels, rows, width = field.shape
    owners = lax.axis_size("row")
    modes_x = 2 * owners
    height = owners * rows
    fwd, inv = height_tables(height)
    spread = jnp.asarray(np.tile(np.eye(BLOCK_CH), (1, channels // BLOCK_CH)), BF16)
    table = jnp.asarray(forward_table(width, modes_x))

    swap = [(0, 1), (1, 0)]
    cut = width // 4
    groups = (((0, 0, width), (1, 0, cut)), ((1, cut, width - cut),))
    (held_first, own_first), (held_second, own_second) = [channel_stats(field, group) for group in groups]
    other_first = lax.ppermute(own_first, "blk", swap)
    other_second = lax.ppermute(own_second, "blk", swap)
    first, part = forward_rows(forward_first, held_first, gain, own_first, other_first, table, owners)
    send = forward_rows(
        forward_second, held_second, gain, own_second, other_second, table, owners, (first, part)
    )
    columns = exchange(send)
    filtered = filter_columns(
        columns, jnp.asarray(fwd), jnp.asarray(inv), spread, w_first, b_first, w_second, b_second
    )
    colfield = exchange(filtered)
    return inverse_rows(colfield, jnp.asarray(inverse_table(width, modes_x)))


def solution(mesh):
    return jax.shard_map(
        local,
        mesh=mesh,
        in_specs=(P(None, "blk", "row", None), P("blk"), P(), P(), P(), P()),
        out_specs=P(None, "blk", "row", None),
        check_vma=False,
    )
```

```python
import functools
import math

import jax
import jax.numpy as jnp
import ml_dtypes
import numpy as np
from jax import lax
from jax.experimental import pallas as pl
from jax.experimental.pallas import tpu as pltpu
from jax.sharding import PartitionSpec as P

BLOCK_CH = 32
EPS = 1e-05
SHRINK = 0.01
BF16 = jnp.bfloat16
F32 = jnp.float32
MIB = 1 << 20


def _angles(first, second, count):
    phase = np.mod(np.outer(first, second), count)
    return phase.astype(np.float32) * np.float32(2.0 * math.pi / count)


def _bf16(values):
    return np.asarray(values, np.float32).astype(ml_dtypes.bfloat16)


def mode_order(modes):
    return np.arange(modes).reshape(-1, 2).T.reshape(-1)


def forward_table(count, modes):
    t = _angles(np.arange(count), mode_order(modes), count)
    scale = np.float32(1.0 / math.sqrt(count))
    return _bf16(np.concatenate([np.cos(t) * scale, -np.sin(t) * scale], axis=1))


def inverse_table(count, modes):
    order = mode_order(modes)
    t = _angles(order, np.arange(count), count)
    weight = np.where(order == 0, 1.0, 2.0)[:, None].astype(np.float32)
    weight = weight * np.float32(1.0 / math.sqrt(count))
    both = np.stack([np.cos(t) * weight, -np.sin(t) * weight])
    both = both.reshape(2, 2, modes // 2, count).transpose(1, 0, 2, 3)
    return _bf16(both.reshape(2 * modes, count))


def height_tables(height):
    quarter = height // 4
    s = _angles(np.arange(quarter + 1), np.arange(height), height)
    scale = np.float32(1.0 / math.sqrt(height))
    cosine, sine = np.cos(s) * scale, np.sin(s) * scale
    last = np.zeros((16, height), np.float32)
    last[0], last[1] = cosine[quarter], sine[quarter]
    forward = np.concatenate([cosine[:quarter], sine[:quarter], last], axis=0)
    inverse = np.concatenate([cosine[:quarter].T, sine[:quarter].T], axis=1)
    return _bf16(forward), _bf16(inverse)


STEP = 16


def copies_of(segments, x_ref, held_refs, sems):
    found = []
    taken = 0
    for (which, first, lanes), ref in zip(segments, held_refs):
        channels, _, width = x_ref.shape[1], x_ref.shape[2], x_ref.shape[3]
        size = STEP * max(1, width // lanes)
        copies = []
        for c in range(0, channels, size):
            part = pl.ds(c, size)
            source = x_ref.at[which, part, :, pl.ds(first, lanes)]
            copies.append(pltpu.make_async_copy(source, ref.at[part], sems.at[taken]))
            taken += 1
        found.append((copies, size))
    return found


def stats_kernel(segments, x_ref, *refs):
    held_refs = refs[: len(segments)]
    stat_ref, pivot_s, first_s, second_s, sems = refs[len(segments) :]
    channels = x_ref.shape[1]
    rows = x_ref.shape[2]
    segment_copies = copies_of(segments, x_ref, held_refs, sems)
    for copies, _ in segment_copies:
        for copy in copies:
            copy.start()
    base = 0
    for (_, _, lanes), ref, (copies, size) in zip(segments, held_refs, segment_copies):
        wide = 512 if lanes % 512 == 0 else min(256, lanes)
        for at in range(0, channels, STEP):
            if at % size == 0:
                copies[at // size].wait()
            for lane in range(0, lanes, wide):
                there = slice(lane, lane + wide)
                here = slice(base + lane, base + lane + wide)
                if at == 0:
                    pivot = jnp.zeros((rows, wide), F32)
                    for c in range(STEP):
                        pivot = pivot + ref[c, :, there].astype(F32)
                    pivot = (pivot * (1.0 / STEP)).astype(BF16)
                    pivot_s[:, here] = pivot
                    first = jnp.zeros((rows, wide), F32)
                    second = jnp.zeros((rows, wide), F32)
                else:
                    pivot, first, second = pivot_s[:, here], first_s[:, here], second_s[:, here]
                for c in range(at, at + STEP, 2):
                    one = ref[c, :, there] - pivot
                    two = ref[c + 1, :, there] - pivot
                    one, two = one.astype(F32), two.astype(F32)
                    first = first + (one + two)
                    second = second + (one * one + two * two)
                if at + STEP < channels:
                    first_s[:, here], second_s[:, here] = first, second
                else:
                    offset = first * (1.0 / channels)
                    mean = pivot.astype(F32) + offset
                    high = mean.astype(BF16)
                    stat_ref[0, :, here] = high
                    stat_ref[1, :, here] = (mean - high.astype(F32)).astype(BF16)
                    stat_ref[2, :, here] = jnp.maximum(second - first * offset, 0.0).astype(BF16)
        base += lanes


def channel_stats(field, segments):
    _, channels, rows, width = field.shape
    total = sum(lanes for _, _, lanes in segments)
    count = sum(channels // (STEP * max(1, width // lanes)) for _, _, lanes in segments)
    vmem = pl.BlockSpec(memory_space=pltpu.VMEM)
    *held, stat = pl.pallas_call(
        functools.partial(stats_kernel, segments),
        in_specs=[pl.BlockSpec(memory_space=pltpu.HBM)],
        out_specs=[vmem] * (len(segments) + 1),
        out_shape=[jax.ShapeDtypeStruct((channels, rows, lanes), BF16) for _, _, lanes in segments]
        + [jax.ShapeDtypeStruct((3, rows, total), BF16)],
        scratch_shapes=[
            pltpu.VMEM((rows, total), BF16),
            pltpu.VMEM((rows, total), F32),
            pltpu.VMEM((rows, total), F32),
            pltpu.SemaphoreType.DMA((count,)),
        ],
        compiler_params=pltpu.CompilerParams(vmem_limit_bytes=16 * MIB),
        cost_estimate=pl.CostEstimate(
            flops=5 * channels * rows * total, bytes_accessed=2 * channels * rows * total, transcendentals=0
        ),
        name="channel_stats",
    )(pltpu.with_memory_space_constraint(field, pltpu.HBM))
    return held, stat


def normalizer(own_ref, other_ref, here, channels):
    own_mean = own_ref[0, :, here].astype(F32) + own_ref[1, :, here].astype(F32)
    other_mean = other_ref[0, :, here].astype(F32) + other_ref[1, :, here].astype(F32)
    delta = own_mean - other_mean
    moment = own_ref[2, :, here].astype(F32) + other_ref[2, :, here].astype(F32) + delta * delta * (channels * 0.5)
    return (own_mean + other_mean) * 0.5, lax.rsqrt(moment * (0.5 / channels) + EPS)


def project(x_ref, stats, table_ref, first_row, pitch, add_ref, spec_ref, chan_block=32):
    channels, rows, lanes = x_ref.shape
    parts, _, half = spec_ref.shape
    mean, scale = stats
    table = table_ref[first_row : first_row + lanes, :]
    for first in range(0, channels, chan_block):
        field = x_ref[first : first + chan_block].astype(F32)
        normed = ((field - mean[None]) * scale[None]).astype(BF16)
        spec = jnp.dot(normed.reshape(chan_block * rows, lanes), table, preferred_element_type=F32)
        for c in range(chan_block):
            start = (first + c) * pitch
            for p in range(parts):
                value = spec[c * rows : (c + 1) * rows, p * half : (p + 1) * half]
                if add_ref is not None:
                    value = value + add_ref[p, start : start + rows, :]
                spec_ref[p, start : start + rows, :] = value
        yield


def hand_out(gain_ref, spec_s, turn_s, slice_ref, rows, pitch, beside=()):
    parts, _, half = spec_s.shape
    channels = turn_s.shape[-1]
    owners = slice_ref.shape[0]
    beside = iter(beside)
    for h in range(rows):
        if h % 4 == 0:
            next(beside, None)
        for p in range(parts):
            turned = spec_s[p, pl.ds(h, channels, stride=pitch), :].T * gain_ref[...]
            turn_s[pl.ds(p * half * pitch + h, half, stride=pitch), :] = turned
    for _ in beside:
        pass
    for r in range(2):
        for kk in range(2):
            for d in range(owners):
                start = ((r * 2 + kk) * owners + d) * pitch
                slice_ref[d, r * rows : (r + 1) * rows, kk * channels : (kk + 1) * channels] = turn_s[
                    start : start + rows, :
                ].astype(BF16)


def forward_first(pitch, x_ref, early_ref, gain_ref, own_ref, other_ref, table_ref, first_ref, part_ref, spec_s, turn_s):
    channels, rows, width = x_ref.shape
    cut = early_ref.shape[2]
    stats = normalizer(own_ref, other_ref, slice(0, width), channels)
    for _ in project(x_ref, stats, table_ref, 0, pitch, None, spec_s):
        pass
    stats = normalizer(own_ref, other_ref, slice(width, width + cut), channels)
    early = project(early_ref, stats, table_ref, 0, pitch, None, part_ref)
    hand_out(gain_ref, spec_s, turn_s, first_ref, rows, pitch, early)


def forward_second(
    pitch, x_ref, gain_ref, own_ref, other_ref, table_ref, first_ref, part_ref, send_ref, spec_s, turn_s, sem
):
    copy = pltpu.make_async_copy(first_ref, send_ref.at[0], sem)
    copy.start()
    channels, rows, lanes = x_ref.shape
    cut = table_ref.shape[0] - lanes
    stats = normalizer(own_ref, other_ref, slice(0, lanes), channels)
    for _ in project(x_ref, stats, table_ref, cut, pitch, part_ref, spec_s):
        pass
    hand_out(gain_ref, spec_s, turn_s, send_ref.at[1], rows, pitch)
    copy.wait()


def forward_rows(kernel, held, gain, own, other, table, owners, more=()):
    channels, rows, _ = held[0].shape
    width, two_k = table.shape
    pitch = rows + 8
    vmem = pl.BlockSpec(memory_space=pltpu.VMEM)
    one = (owners, 2 * rows, 2 * channels)
    part = jax.ShapeDtypeStruct((2, (channels + 1) * pitch, two_k // 2), F32)
    lanes = sum(x.shape[2] for x in held)
    return pl.pallas_call(
        functools.partial(kernel, pitch),
        in_specs=[vmem] * (len(held) + 4 + len(more)),
        out_specs=vmem if more else [vmem, vmem],
        out_shape=jax.ShapeDtypeStruct((2,) + one, BF16) if more else [jax.ShapeDtypeStruct(one, BF16), part],
        scratch_shapes=[
            pltpu.VMEM((2, (channels + 1) * pitch, two_k // 2), F32),
            pltpu.VMEM(((two_k + 1) * pitch, channels), F32),
        ]
        + [pltpu.SemaphoreType.DMA] * (1 if more else 0),
        compiler_params=pltpu.CompilerParams(vmem_limit_bytes=24 * MIB),
        cost_estimate=pl.CostEstimate(
            flops=2 * channels * rows * lanes * two_k, bytes_accessed=2 * channels * rows * lanes, transcendentals=0
        ),
        name="norm_and_row_dft",
    )(*held, gain.reshape(1, channels), own, other, table, *more)


def block_diagonal(weights, spread, lanes):
    tiled = jnp.dot(weights, spread, preferred_element_type=F32)
    row = lax.broadcasted_iota(jnp.int32, (lanes, lanes), 0) // BLOCK_CH
    col = lax.broadcasted_iota(jnp.int32, (lanes, lanes), 1) // BLOCK_CH
    return jnp.where(row == col, tiled, 0.0)


def fill_weights(w_ref, group, spread, big, lanes, turned=None):
    mine = slice(group * lanes, (group + 1) * lanes)
    real = block_diagonal(w_ref[0, mine, :], spread, lanes)
    imag = block_diagonal(w_ref[1, mine, :], spread, lanes)
    for target, shift in ((big, 0), (turned, lanes // 2)):
        if target is not None:
            re = pltpu.roll(real, shift, 1) if shift else real
            im = pltpu.roll(imag, shift, 1) if shift else imag
            target[:lanes, :lanes] = re.astype(BF16)
            target[:lanes, lanes:] = im.astype(BF16)
            target[lanes:, :lanes] = (-im).astype(BF16)
            target[lanes:, lanes:] = re.astype(BF16)


def bias_row(b_ref, group, lanes, shift=0):
    mine = slice(group * lanes, (group + 1) * lanes)
    both = [b_ref[0:1, mine], b_ref[1:2, mine]]
    if shift:
        both = [pltpu.roll(b, shift, 1) for b in both]
    return jnp.concatenate(both, axis=1)


def filter_kernel(x_ref, fwd_ref, inv_ref, spread_ref, w1_ref, b1_ref, w2_ref, b2_ref, out_ref, big1, big2, big2_turned, spec_s, packed):
    groups, owners, two_rows, wide = x_ref.shape
    rows = two_rows // 2
    lanes = wide // 2
    height = owners * rows
    quarter = height // 4
    top = lax.broadcasted_iota(jnp.int32, (quarter, lanes), 0) == 0
    turn = lax.broadcasted_iota(jnp.int32, (8, 1), 0) % 4
    norm = 1.0 / math.sqrt(height)
    last_cos = jnp.where(turn == 0, norm, jnp.where(turn == 2, -norm, 0.0))
    last_sin = jnp.where(turn == 1, norm, jnp.where(turn == 3, -norm, 0.0))
    real_part = lambda kk: slice(kk * lanes, (kk + 1) * lanes)

    def transform(group):
        real_in = x_ref[group, :, :rows, :].reshape(height, wide)
        imag_in = x_ref[group, :, rows:, :].reshape(height, wide)
        from_real = jnp.dot(fwd_ref[...], real_in, preferred_element_type=F32)
        from_imag = jnp.dot(fwd_ref[...], imag_in, preferred_element_type=F32)
        last = slice(2 * quarter, 2 * quarter + 1)
        last_sine = slice(2 * quarter + 1, 2 * quarter + 2)
        for kk in range(2):
            part = real_part(kk)
            cos_re, sin_re = from_real[:quarter, part], from_real[quarter : 2 * quarter, part]
            cos_im, sin_im = from_imag[:quarter, part], from_imag[quarter : 2 * quarter, part]
            last_re = from_real[last, part] - from_imag[last_sine, part]
            last_im = from_imag[last, part] + from_real[last_sine, part]
            spec_s[group, kk, :quarter, :lanes] = (cos_re + sin_im).astype(BF16)
            spec_s[group, kk, :quarter, lanes:] = (cos_im - sin_re).astype(BF16)
            spec_s[group, kk, quarter:, :lanes] = jnp.where(top, last_re, cos_re - sin_im).astype(BF16)
            spec_s[group, kk, quarter:, lanes:] = jnp.where(top, last_im, cos_im + sin_re).astype(BF16)

    def mix(group):
        values, extras = [], []
        for kk in range(2):
            shift = kk * (lanes // 2)
            second = (big2 if kk == 0 else big2_turned)[group]
            hidden = jnp.dot(spec_s[group, kk], big1[group], preferred_element_type=F32) + bias_row(b1_ref, group, lanes)
            hidden = jnp.maximum(hidden, 0.0).astype(BF16)
            mixed = jnp.dot(hidden, second, preferred_element_type=F32) + bias_row(b2_ref, group, lanes, shift)
            kept = mixed - jnp.clip(mixed, -SHRINK, SHRINK)
            plus_re, plus_im = kept[:quarter, :lanes], kept[:quarter, lanes:]
            minus_re, minus_im = kept[quarter:, :lanes], kept[quarter:, lanes:]
            last_re, last_im = minus_re[0:1], minus_im[0:1]
            minus_re = jnp.where(top, 0.0, minus_re)
            minus_im = jnp.where(top, 0.0, minus_im)
            values.append([plus_re + minus_re, plus_im + minus_im, minus_im - plus_im, plus_re - minus_re])
            extras.append([last_cos * last_re + last_sin * last_im, last_cos * last_im - last_sin * last_re])

        def halves(zero, one):
            low = lax.broadcasted_iota(jnp.int32, zero.shape, 1) < lanes // 2
            return jnp.where(low, zero, one), jnp.where(low, one, zero)

        for i, (zero, one) in enumerate(zip(*values)):
            for half, value in enumerate(halves(zero, one)):
                start = (i % 2) * wide + half * lanes
                packed[group, (i // 2) * quarter : (i // 2 + 1) * quarter, start : start + lanes] = value.astype(BF16)
        return jnp.concatenate([part for zero, one in zip(*extras) for part in halves(zero, one)], axis=1)

    def invert(group, extra):
        column = jnp.dot(inv_ref[...], packed[group], preferred_element_type=F32)
        column = (column.reshape(height // 8, 8, 2 * wide) + extra[None]).astype(BF16)
        column = column.reshape(height, 2 * wide)
        out_ref[group, :, :rows, :] = column[:, :wide].reshape(owners, rows, wide)
        out_ref[group, :, rows:, :] = column[:, wide:].reshape(owners, rows, wide)

    for group in range(groups):
        fill_weights(w1_ref, group, spread_ref[...], big1.at[group], lanes)
        fill_weights(w2_ref, group, spread_ref[...], big2.at[group], lanes, big2_turned.at[group])
    for group in range(groups):
        transform(group)
    extra = [mix(group) for group in range(groups)]
    for group in range(groups):
        invert(group, extra[group])


def filter_columns(received, fwd, inv, spread, w_first, b_first, w_second, b_second):
    groups, owners, two_rows, wide = received.shape
    height = owners * two_rows // 2
    vmem = pl.BlockSpec(memory_space=pltpu.VMEM)

    def flat(w):
        return w.reshape(2, -1, BLOCK_CH)

    return pl.pallas_call(
        filter_kernel,
        in_specs=[vmem] * 8,
        out_specs=vmem,
        out_shape=jax.ShapeDtypeStruct(received.shape, BF16),
        scratch_shapes=[
            pltpu.VMEM((groups, wide, wide), BF16),
            pltpu.VMEM((groups, wide, wide), BF16),
            pltpu.VMEM((groups, wide, wide), BF16),
            pltpu.VMEM((groups, 2, height // 2, wide), BF16),
            pltpu.VMEM((groups, height // 2, 2 * wide), BF16),
        ],
        compiler_params=pltpu.CompilerParams(vmem_limit_bytes=40 * MIB),
        cost_estimate=pl.CostEstimate(
            flops=2 * groups * height * wide * 3 * height, bytes_accessed=8 * MIB, transcendentals=0
        ),
        name="column_filter",
    )(received, fwd, inv, spread, flat(w_first), b_first, flat(w_second), b_second)


def inverse_kernel(chan_block, pitch, x_ref, table_ref, out_ref, turn_s, spec_s, done_s, sems):
    slices, owners, two_rows, wide = x_ref.shape
    rows = two_rows // 2
    lanes = wide // 2
    part = lanes // 2
    copies = []
    for which in range(slices):
        for half in range(2):
            for r in range(2):
                for d in range(owners):
                    start = (r * owners + d) * pitch
                    turn_s[half, start : start + rows, :] = x_ref[
                        which, d, r * rows : (r + 1) * rows, half * lanes : (half + 1) * lanes
                    ].astype(F32)
            for h in range(rows):
                turned = turn_s[half, pl.ds(h, 2 * owners, stride=pitch), :].T
                for place in range(2):
                    kk = place if half == 0 else 1 - place
                    spec_s[kk, pl.ds(half * part * pitch + h, part, stride=pitch), :] = turned[
                        place * part : (place + 1) * part
                    ]
            for first in range(half * part, (half + 1) * part, chan_block):
                spec = []
                for c in range(first, first + chan_block):
                    start = c * pitch
                    both = [spec_s[kk, start : start + rows, :].astype(BF16) for kk in range(2)]
                    spec.append(jnp.concatenate(both, axis=1))
                mixed = jnp.dot(jnp.concatenate(spec, axis=0), table_ref[...], preferred_element_type=F32)
                block = pl.ds(first, chan_block)
                done_s[which, block] = mixed.astype(BF16).reshape(chan_block, rows, -1)
                copies.append(
                    pltpu.make_async_copy(done_s.at[which, block], out_ref.at[which, block], sems.at[len(copies)])
                )
                copies[-1].start(priority=len(copies) % 2)
    for copy in copies:
        copy.wait()


def inverse_rows(received, table):
    slices, owners, two_rows, wide = received.shape
    rows = two_rows // 2
    channels = wide // 2
    two_k, width = table.shape
    chan_block = min(16, channels)
    pitch = rows + 8
    vmem = pl.BlockSpec(memory_space=pltpu.VMEM)
    return pl.pallas_call(
        functools.partial(inverse_kernel, chan_block, pitch),
        in_specs=[vmem, vmem],
        out_specs=pl.BlockSpec(memory_space=pltpu.HBM),
        out_shape=jax.ShapeDtypeStruct((slices, channels, rows, width), BF16),
        scratch_shapes=[
            pltpu.VMEM((2, (two_k // 2 + 1) * pitch, channels), F32),
            pltpu.VMEM((2, (channels + 1) * pitch, two_k // 2), F32),
            pltpu.VMEM((slices, channels, rows, width), BF16),
            pltpu.SemaphoreType.DMA((slices * channels // chan_block,)),
        ],
        compiler_params=pltpu.CompilerParams(vmem_limit_bytes=40 * MIB),
        cost_estimate=pl.CostEstimate(
            flops=2 * slices * channels * rows * width * two_k,
            bytes_accessed=2 * slices * channels * rows * width,
            transcendentals=0,
        ),
        name="inverse_row_dft",
    )(received, table)


def exchange(blocks):
    shape = blocks.shape
    flat = blocks.reshape((shape[0] * shape[1],) + shape[2:])
    flat = lax.all_to_all(flat, ("blk", "row"), split_axis=0, concat_axis=0, tiled=True)
    return flat.reshape(shape)


def local(field, gain, w_first, b_first, w_second, b_second):
    slices, channels, rows, width = field.shape
    owners = lax.axis_size("row")
    modes_x = 2 * owners
    height = owners * rows
    fwd, inv = height_tables(height)
    spread = jnp.asarray(np.tile(np.eye(BLOCK_CH), (1, channels // BLOCK_CH)), BF16)
    table = jnp.asarray(forward_table(width, modes_x))

    swap = [(0, 1), (1, 0)]
    cut = width // 4
    groups = (((0, 0, width), (1, 0, cut)), ((1, cut, width - cut),))
    (held_first, own_first), (held_second, own_second) = [channel_stats(field, group) for group in groups]
    other_first = lax.ppermute(own_first, "blk", swap)
    other_second = lax.ppermute(own_second, "blk", swap)
    first, part = forward_rows(forward_first, held_first, gain, own_first, other_first, table, owners)
    send = forward_rows(
        forward_second, held_second, gain, own_second, other_second, table, owners, (first, part)
    )
    columns = exchange(send)
    filtered = filter_columns(
        columns, jnp.asarray(fwd), jnp.asarray(inv), spread, w_first, b_first, w_second, b_second
    )
    colfield = exchange(filtered)
    return inverse_rows(colfield, jnp.asarray(inverse_table(width, modes_x)))


def solution(mesh):
    return jax.shard_map(
        local,
        mesh=mesh,
        in_specs=(P(None, "blk", "row", None), P("blk"), P(), P(), P(), P()),
        out_specs=P(None, "blk", "row", None),
        check_vma=False,
    )
```
